32 devices in a mesh: dp: 8 (over z, core), expert: 4 (over y, x).
Axes of the slice: x: 2, y: 2, z: 4, core: 2. Of those that a mesh axis runs over, the one named last changes fastest.
Arguments:
- ssm_state: bfloat16 [256, 16, 4096], P('expert', None, 'dp'), may hold values from -6 to 6
- conv_state: bfloat16 [256, 3, 4096], P('expert', None, 'dp'), may hold values from -6 to 6
- new_slot: int32 [256], replicated, may hold values from 0 to 255, as said below
- conv_input: bfloat16 [256, 4096], P('expert', 'dp'), may hold values from -6 to 6
- gate_input: bfloat16 [256, 4096], P('expert', 'dp'), may hold values from -6 to 6
- conv_weight: float32 [4, 4096], P(None, 'dp'), may hold values from -3 to 3
- conv_bias: float32 [4096], P('dp'), may hold values from -3 to 3
- x_proj_weight: bfloat16 [4096, 288], P('dp'), may hold values from -0.09375 to 0.09375
- step_weight: bfloat16 [256, 4096], P(None, 'dp'), may hold values from -0.375 to 0.375
- step_bias: float32 [4096], P('dp'), may hold values from -3 to -0.5
- decay_log: float32 [16, 4096], P(None, 'dp'), may hold values from 0 to 2
- skip_gain: float32 [4096], P('dp'), may hold values from 0.5 to 1.5
- out_proj_weight: bfloat16 [4096, 4096], P('dp', 'expert'), may hold values from -0.09375 to 0.09375
- residual: bfloat16 [256, 4096], P(None, 'expert'), may hold values from -6 to 6
- norm_gain: float32 [4096], replicated, may hold values from 0.1 to 1.9
- routes: int32 [256, 2], replicated, may hold values from 0 to 3, all different within a row; in each aligned block of 64 rows (0 to 63, 64 to 127, ...) at most 64 rows name the same one
- gate_weight: float32 [256, 2], replicated, may hold values from 0.1 to 0.9
- expert_gate: bfloat16 [4, 4096, 7168], P('expert', None, 'dp'), may hold values from -0.09375 to 0.09375
- expert_up: bfloat16 [4, 4096, 7168], P('expert', None, 'dp'), may hold values from -0.09375 to 0.09375
- expert_down: bfloat16 [4, 7168, 4096], P('expert', 'dp'), may hold values from -0.0625 to 0.0625
Outputs:
- ssm_new: bfloat16 [256, 16, 4096], P('expert', None, 'dp')
- conv_new: bfloat16 [256, 3, 4096], P('expert', None, 'dp')
- layer_out: bfloat16 [256, 4096], P(None, 'expert')
The draws below stay inside these ranges and needn't reach their ends.
Inputs may be any that keep to these rules, and one draw needn't show every extreme that they name: new_slot is a permutation of the 256 slots; slot s belongs to expert index s // 64. Of the 64 old slots of one expert index, at most 32 get new slots of any one expert index, and exactly 32 those of some expert index; every expert index sends the same multiset of such counts. `routes`: each row names 2 different experts; within each aligned block of 64 rows (the rows of one expert index) no expert is named by more than 64 rows, a bound that some block reaches.
All inputs are finite; a program needn't handle non-finite values.
Results may differ from the reference program's by a relative error of at most 0.012.
Values may be sent and summed in bfloat16 or wider, within the bound.
No kernel may reach another device: no remote copies, remote signals or barrier semaphores. Data moves between devices by JAX's collectives and lax.ppermute only.
A program may use at most 128 MiB of HBM per device.

```python
import math
import jax
import jax.numpy as jnp
import numpy as np
from jax import lax

D = 4096
RK = 256
NS = 16
KC = 4
TOPK = 2
DI = 4096
FF = 7168
REQ_DEV = 64
REQ = 256
EXPERTS = 4
CAP = 64


def draw_new_slot(key, part):
    row_count = REQ_DEV
    owners = REQ // REQ_DEV
    base = row_count // owners
    keys = jax.random.split(key, 6)
    pairing = jax.random.permutation(keys[0], owners)
    amplitude = jax.random.randint(keys[1], (owners // 2,), 0, base + 1).astype(jnp.int32)
    amplitude = amplitude.at[0].set(base)
    weights = jnp.zeros((owners,), jnp.int32)
    weights = weights.at[pairing[0::2]].set(base + amplitude)
    weights = weights.at[pairing[1::2]].set(base - amplitude)
    source_perm = jax.random.permutation(keys[2], owners)
    target_perm = jax.random.permutation(keys[3], owners)
    counts = weights[(target_perm[None, :] - source_perm[:, None]) % owners]
    ends = jnp.cumsum(counts, axis=1)
    starts = ends - counts
    places = jnp.arange(row_count, dtype=jnp.int32)
    target = jnp.sum((places[None, :, None] >= ends[:, None, :]).astype(jnp.int32), axis=2)
    within = places[None, :] - jnp.take_along_axis(starts, target, axis=1)
    offsets = jnp.cumsum(counts, axis=0) - counts
    position = jnp.take_along_axis(offsets, target, axis=1) + within
    shuffles = jax.vmap(lambda sub: jax.random.permutation(sub, row_count))(jax.random.split(keys[4], owners))
    new_place = shuffles[target, position]
    slot_sorted = target * row_count + new_place
    row_perm = jax.vmap(lambda sub: jax.random.permutation(sub, row_count))(jax.random.split(keys[5], owners))
    result = jnp.zeros((owners, row_count), jnp.int32)
    result = result.at[jnp.arange(owners)[:, None], row_perm].set(slot_sorted.astype(jnp.int32))
    return result.reshape(REQ)


def shard_levels(rng, shape, cuts, low, largest):
    factor_of = 1.0
    for axis_at, blocks in cuts:
        draws = jax.random.uniform(jax.random.fold_in(jax.random.fold_in(rng, 6), axis_at), (blocks,), jnp.float32, low / len(cuts), largest / len(cuts))
        factor_of = factor_of * jnp.repeat(jnp.exp(draws), shape[axis_at] // blocks).reshape((-1,) + (1,) * (len(shape) - 1 - axis_at))
    return factor_of


def routed_block(own_key, own, number, rows, number_of, top, most, skew):
    order = jax.random.permutation(own_key, number_of)
    heavy_load, ordinary = shares(number_of, rows * top, most, skew, True), shares(number_of, rows * top, most, skew, False)
    places = jnp.arange(number_of)

    def named(sizes, turn):
        used = int((sizes > 0).sum())
        fixed = max(1, used // 4)
        passed = fixed + (places - fixed + turn * (used - fixed)) % max(1, number_of - fixed)
        return jnp.zeros((number_of,), jnp.int32).at[order[jnp.where(places < fixed, places, passed)]].set(jnp.asarray(sizes, jnp.int32))

    sizes = jnp.where(number % 4 == 0, named(heavy_load, number // 4), named(ordinary, number - number // 4 - 1))
    mixed = jax.random.permutation(jax.random.fold_in(own, 3), number_of)
    giver, sink = mixed[0:number_of // 2 * 2:2], mixed[1:number_of // 2 * 2:2]
    slack = jnp.minimum(sizes[giver] - 1, most - sizes[sink]) // 2
    slack = jnp.where((giver == order[0]) | (sink == order[0]) | (sizes[sink] == 0), 0, jnp.maximum(slack, 0))
    passed = jax.random.randint(jax.random.fold_in(own, 4), (number_of // 2,), 0, 1 << 20) % (slack + 1)
    sizes = sizes.at[giver].add(-passed).at[sink].add(passed)
    members = jnp.searchsorted(jnp.cumsum(sizes), jnp.arange(rows * top), side="right").astype(jnp.int32)
    grid = members.reshape(top, rows).T
    grid = grid[jax.random.permutation(jax.random.fold_in(own, 1), rows)]
    turn = jax.random.randint(jax.random.fold_in(own, 2), (rows, 1), 0, top)
    return jnp.take_along_axis(grid, (jnp.arange(top)[None, :] + turn) % top, axis=1)


def shares(amount, total, bound, skew, full):
    portions = [(1 << 20) // math.isqrt(grade ** skew) + 1 for grade in range(1, amount + 1)]
    largest = bound if full else min(bound, max(-(-total // amount), total * portions[0] // sum(portions)))
    least = 1 if total - largest >= amount - 1 else 0
    holding, rest = [largest] + [least] * (amount - 1), total - largest - least * (amount - 1)
    while rest > 0:
        movable = [i for i in range(1, amount) if holding[i] < largest] or [i for i in range(1, amount) if holding[i] < bound]
        whole, remaining = sum([portions[i] for i in movable]), rest
        for i in movable:
            more = min(bound - holding[i], max(1, remaining * portions[i] // whole), rest)
            holding[i] = holding[i] + more
            rest = rest - more
    return np.array(holding)


def scatter_about(key, extent, deviation, most, cuts=(), kind=jnp.bfloat16):
    entries = deviation * jax.random.normal(key, extent, jnp.float32)
    if cuts:
        entries = entries * shard_levels(key, extent, cuts, -0.22, 0.18)
    return jnp.clip(entries, -most, most).astype(kind)


def setup_inputs(seed: int = 0) -> dict:
    key_list = jax.random.split(jax.random.key(seed), 21)
    ssm_state = scatter_about(key_list[0], (REQ, NS, DI), 1.0, 6.0, ((0, 4), (2, 8)))
    conv_state = scatter_about(key_list[1], (REQ, KC - 1, DI), 1.0, 6.0, ((0, 4), (2, 8)))
    new_slot = draw_new_slot(jax.random.fold_in(key_list[20], 71), 0)
    conv_input = scatter_about(key_list[3], (REQ, DI), 1.0, 6.0, ((0, 4), (1, 8)))
    gate_input = scatter_about(key_list[4], (REQ, DI), 1.0, 6.0, ((0, 4), (1, 8)))
    conv_weight = scatter_about(key_list[5], (KC, DI), KC ** -0.5, 3.0, ((1, 8),), jnp.float32)
    conv_bias = scatter_about(key_list[6], (DI,), 0.5, 3.0, ((0, 8),), jnp.float32)
    x_proj_weight = scatter_about(key_list[7], (DI, RK + 2 * NS), DI ** -0.5, 0.09375, ((0, 8),))
    step_weight = scatter_about(key_list[8], (RK, DI), RK ** -0.5, 0.375, ((1, 8),))
    step_bias = jnp.clip(-3.0 + 2.5 * jax.random.uniform(key_list[9], (DI,), jnp.float32) ** shard_levels(key_list[9], (DI,), ((0, 8),), -0.2, 0.2), -3.0, -0.5)
    decay_log = jnp.clip(2.0 * jax.random.uniform(key_list[10], (NS, DI), jnp.float32) ** shard_levels(key_list[10], (NS, DI), ((1, 8),), -0.2, 0.2), 0.0, 2.0)
    skip_gain = jnp.clip(0.5 + 1.0 * jax.random.uniform(key_list[11], (DI,), jnp.float32) ** shard_levels(key_list[11], (DI,), ((0, 8),), -0.2, 0.2), 0.5, 1.5)
    out_proj_weight = scatter_about(key_list[12], (DI, D), DI ** -0.5, 0.09375, ((0, 8), (1, 4)))
    residual = scatter_about(key_list[13], (REQ, D), 1.0, 6.0, ((1, 4),))
    norm_gain = jnp.clip(1.0 + 0.18 * jax.random.normal(key_list[14], (D,), jnp.float32), 0.1, 1.9)
    routes_keys = jax.random.split(jax.random.fold_in(key_list[15], 1), REQ // REQ_DEV)
    routes_turns = jax.random.permutation(jax.random.fold_in(key_list[15], 3), REQ // REQ_DEV)
    routes = jax.vmap(lambda own, number: routed_block(jax.random.fold_in(key_list[15], 2), own, number, REQ_DEV, EXPERTS, TOPK, CAP, 2))(routes_keys, routes_turns).reshape((REQ, TOPK))
    gate_weight = jnp.clip(jax.random.uniform(key_list[16], (REQ, TOPK), jnp.float32, 0.1, 0.9), 0.1, 0.9)
    expert_gate = scatter_about(key_list[17], (EXPERTS, D, FF), D ** -0.5, 0.09375, ((0, 4), (2, 8)))
    expert_up = scatter_about(key_list[18], (EXPERTS, D, FF), D ** -0.5, 0.09375, ((0, 4), (2, 8)))
    expert_down = scatter_about(key_list[19], (EXPERTS, FF, D), FF ** -0.5, 0.0625, ((0, 4), (1, 8)))
    return {"ssm_state": ssm_state, "conv_state": conv_state, "new_slot": new_slot, "conv_input": conv_input, "gate_input": gate_input, "conv_weight": conv_weight, "conv_bias": conv_bias, "x_proj_weight": x_proj_weight, "step_weight": step_weight, "step_bias": step_bias, "decay_log": decay_log, "skip_gain": skip_gain, "out_proj_weight": out_proj_weight, "residual": residual, "norm_gain": norm_gain, "routes": routes, "gate_weight": gate_weight, "expert_gate": expert_gate, "expert_up": expert_up, "expert_down": expert_down}


def reference(ssm_state, conv_state, new_slot, conv_input, gate_input, conv_weight, conv_bias, x_proj_weight, step_weight, step_bias, decay_log, skip_gain, out_proj_weight, residual, norm_gain, routes, gate_weight, expert_gate, expert_up, expert_down):
    moved_ssm = jnp.zeros_like(ssm_state).at[new_slot].set(ssm_state)
    moved_conv = jnp.zeros_like(conv_state).at[new_slot].set(conv_state)
    window = jnp.concatenate([moved_conv, conv_input[:, None, :]], axis=1)
    conv_new = window[:, 1:, :]
    conv_sum = lax.optimization_barrier(jnp.sum(window.astype(jnp.float32) * conv_weight[None, :, :], axis=1)) + conv_bias[None, :]
    activated = jax.nn.silu(conv_sum).astype(jnp.bfloat16)
    projected = jnp.dot(activated, x_proj_weight, preferred_element_type=jnp.float32)
    step_low = projected[:, :RK]
    b_coef = projected[:, RK:RK + NS]
    c_coef = projected[:, RK + NS:]
    step_norm = (step_low * lax.rsqrt(lax.optimization_barrier(jnp.mean(step_low * step_low, axis=1, keepdims=True)) + 1e-06)).astype(jnp.bfloat16)
    step_size = jax.nn.softplus(jnp.dot(step_norm, step_weight, preferred_element_type=jnp.float32) + step_bias[None, :])
    act_float = activated.astype(jnp.float32)
    decays = jnp.exp(step_size[:, None, :] * (-jnp.exp(decay_log))[None, :, :])
    states = decays * moved_ssm.astype(jnp.float32) + (step_size * act_float)[:, None, :] * b_coef[:, :, None]
    ssm_new = states.astype(jnp.bfloat16)
    gated_out = ((lax.optimization_barrier(jnp.sum(c_coef[:, :, None] * states, axis=1)) + skip_gain[None, :] * act_float) * jax.nn.silu(gate_input.astype(jnp.float32))).astype(jnp.bfloat16)
    stream = (residual.astype(jnp.float32) + jnp.dot(gated_out, out_proj_weight, preferred_element_type=jnp.float32)).astype(jnp.bfloat16)
    stream_f = stream.astype(jnp.float32)
    normed = (stream_f * lax.rsqrt(lax.optimization_barrier(jnp.mean(stream_f * stream_f, axis=1, keepdims=True)) + 1e-05) * norm_gain[None, :]).astype(jnp.bfloat16)
    limit = REQ // REQ_DEV * CAP

    def one_expert(expert_id):
        chosen = routes == expert_id
        row_weight = lax.optimization_barrier(jnp.sum(jnp.where(chosen, gate_weight, jnp.zeros_like(gate_weight)), axis=1))
        used = jnp.any(chosen, axis=1)
        keys = jnp.where(used, 0, 1).astype(jnp.int32)
        picked = jnp.argsort(keys, stable=True)[:limit].astype(jnp.int32)
        rows_in = normed[picked]
        gate_val = jnp.dot(rows_in, expert_gate[expert_id], preferred_element_type=jnp.float32)
        up_val = jnp.dot(rows_in, expert_up[expert_id], preferred_element_type=jnp.float32)
        hidden = (jax.nn.silu(gate_val) * up_val).astype(jnp.bfloat16)
        result = jnp.dot(hidden, expert_down[expert_id], preferred_element_type=jnp.float32)
        return (picked, result * row_weight[picked][:, None])
    picked_all, contrib = lax.map(one_expert, jnp.arange(EXPERTS, dtype=jnp.int32))
    expert_mix = jnp.zeros((REQ, D), jnp.float32).at[picked_all.reshape(-1)].add(contrib.reshape(-1, D))
    layer_out = (stream_f + expert_mix).astype(jnp.bfloat16)
    return (ssm_new, conv_new, layer_out)
```

```python
import jax
import jax.numpy as jnp
from jax import lax
from jax.sharding import PartitionSpec as P

F32 = jnp.float32
BF16 = jnp.bfloat16


def swap(values, axis, flip):
    size = lax.axis_size(axis)
    return lax.ppermute(values, axis, [(i, i ^ flip) for i in range(size)])


def gather_pairs(values, axis, stride=1):
    count = lax.axis_size(axis) // stride
    return [values] + [swap(values, axis, flip * stride) for flip in range(1, count)]


def scatter_pairs(parts, axis, stride=1):
    total = parts[0].astype(F32)
    for flip in range(1, len(parts)):
        total = total + swap(parts[flip].astype(BF16), axis, flip * stride).astype(F32)
    return total


def dispatch_experts(stream, norm_gain, routes, gate_weight, expert_gate, expert_up, expert_down, row_count, capacity):
    owners = lax.axis_size("expert")
    top_count = routes.shape[1]
    width = stream.shape[1]
    expert_hot = (
        (routes[:, :, None] == jnp.arange(owners)[None, None, :])
        .astype(jnp.int32)
        .reshape(owners, row_count * top_count, owners)
    )
    prior = jnp.sum((jnp.cumsum(expert_hot, axis=1) - expert_hot) * expert_hot, axis=2)
    slot_of = (routes.reshape(owners, row_count * top_count) * capacity + prior).reshape(owners, row_count, top_count)
    matches = slot_of[:, :, :, None] == jnp.arange(owners * capacity)[None, None, None, :]
    dispatch_hot = jnp.any(matches, axis=2).astype(BF16).reshape(owners, row_count, owners, capacity)
    combine_w = jnp.sum(
        jnp.where(matches, gate_weight.reshape(owners, row_count, top_count)[:, :, :, None], 0.0), axis=2
    ).reshape(owners, row_count, owners, capacity)
    outgoing = jnp.einsum(
        "orec,ord->eocd", dispatch_hot, stream.reshape(owners, row_count, width), preferred_element_type=F32
    ).astype(BF16)
    arrived = lax.all_to_all(outgoing, "expert", split_axis=0, concat_axis=3, tiled=True)
    tokens = arrived.reshape(owners * capacity, -1).astype(F32)
    normed = (
        tokens * lax.rsqrt(jnp.mean(tokens * tokens, axis=1, keepdims=True) + 1e-05) * norm_gain[None, :]
    ).astype(BF16)
    gate_val = jnp.dot(normed, expert_gate, preferred_element_type=F32)
    up_val = jnp.dot(normed, expert_up, preferred_element_type=F32)
    hidden = (jax.nn.silu(gate_val) * up_val).astype(BF16)
    partial_out = jnp.dot(hidden, expert_down, preferred_element_type=F32).reshape(owners, capacity, -1)
    summed = lax.psum(partial_out, "dp")
    returned = lax.all_to_all(summed.astype(BF16), "expert", split_axis=2, concat_axis=0, tiled=True).astype(F32)
    expert_mix = jnp.einsum(
        "orec,eocd->ord",
        combine_w,
        returned.reshape(owners, owners, capacity, width),
        precision=lax.Precision.HIGHEST,
        preferred_element_type=F32,
    )
    return (stream.astype(F32) + expert_mix.reshape(-1, width)).astype(BF16)


def body(
    ssm_state,
    conv_state,
    new_slot,
    conv_input,
    gate_input,
    conv_weight,
    conv_bias,
    x_proj_weight,
    step_weight,
    step_bias,
    decay_log,
    skip_gain,
    out_proj_weight,
    residual,
    norm_gain,
    routes,
    gate_weight,
    expert_gate,
    expert_up,
    expert_down,
):
    row_count, state_dim, channels = ssm_state.shape
    owners = lax.axis_size("expert")
    own = lax.axis_index("expert")
    dp_index = lax.axis_index("dp")
    core = dp_index % 2
    plane = dp_index // 2
    planes = lax.axis_size("dp") // 2
    rows = owners * row_count
    half = rows // 2
    chunk = half // planes
    tap_count = conv_weight.shape[0]

    conv_all = jnp.concatenate(gather_pairs(conv_input, "expert"), axis=0)
    tied_gate, conv_all = lax.optimization_barrier((gate_input, conv_all))
    gate_all = jnp.concatenate(gather_pairs(tied_gate, "expert"), axis=0)
    my_slots = lax.dynamic_slice_in_dim(new_slot, own * row_count, row_count)
    near_ids = (
        (jnp.arange(owners) ^ own)[:, None] * row_count + jnp.arange(row_count)[None, :]
    ).reshape(-1)
    pick = (my_slots[:, None] == near_ids[None, :]).astype(BF16)
    conv_in = jnp.dot(pick, conv_all, preferred_element_type=F32)

    conv_sum = (
        jnp.sum(conv_state.astype(F32) * conv_weight[None, : tap_count - 1, :], axis=1)
        + conv_in * conv_weight[tap_count - 1][None, :]
        + conv_bias[None, :]
    )
    activated = jax.nn.silu(conv_sum).astype(BF16)
    projected = jnp.dot(activated, x_proj_weight, preferred_element_type=F32)
    projected = projected + swap(projected, "dp", 1)
    projected = scatter_pairs([projected] * planes, "dp", 2)
    rank_dim = step_weight.shape[0]
    step_low = projected[:, :rank_dim]
    b_coef = projected[:, rank_dim : rank_dim + state_dim]
    c_coef = projected[:, rank_dim + state_dim :]
    step_norm = (
        step_low * lax.rsqrt(jnp.mean(step_low * step_low, axis=1, keepdims=True) + 1e-06)
    ).astype(BF16)
    step_size = jax.nn.softplus(
        jnp.dot(step_norm, step_weight, preferred_element_type=F32) + step_bias[None, :]
    )
    act_float = activated.astype(F32)
    decays = jnp.exp(step_size[:, None, :] * (-jnp.exp(decay_log))[None, :, :])
    states = decays * ssm_state.astype(F32) + (step_size * act_float)[:, None, :] * b_coef[:, :, None]
    gate_in = jnp.dot(pick, gate_all, preferred_element_type=F32)
    gated_out = (
        (jnp.sum(c_coef[:, :, None] * states, axis=1) + skip_gain[None, :] * act_float) * jax.nn.silu(gate_in)
    ).astype(BF16)
    ssm_old = states.astype(BF16)

    gated_all = jnp.concatenate(gather_pairs(gated_out, "expert"), axis=0)
    old_slots = new_slot.reshape(owners, row_count)
    near_slots = jnp.concatenate(
        [lax.dynamic_slice_in_dim(old_slots, own ^ flip, 1, axis=0) for flip in range(owners)], axis=0
    ).reshape(-1)
    order_hot = (jnp.arange(rows)[:, None] == near_slots[None, :]).astype(BF16)
    gated_new = jnp.dot(order_hot, gated_all, preferred_element_type=F32).astype(BF16)
    mix = jnp.dot(gated_new, out_proj_weight, preferred_element_type=F32)

    width = mix.shape[1]
    mix = mix.reshape(2, planes, chunk, width)
    kept = lax.dynamic_index_in_dim(mix, core, 0, keepdims=False)
    sent = lax.dynamic_index_in_dim(mix, 1 - core, 0, keepdims=False)
    mix_half = kept + swap(sent.astype(BF16), "dp", 1).astype(F32)
    mix_chunk = scatter_pairs(
        [lax.dynamic_index_in_dim(mix_half, plane ^ flip, 0, keepdims=False) for flip in range(planes)], "dp", 2
    )
    residual_chunk = lax.dynamic_slice_in_dim(residual, core * half + plane * chunk, chunk, axis=0)
    stream_chunk = (residual_chunk.astype(F32) + mix_chunk).astype(BF16)
    stream_half = jnp.concatenate(gather_pairs(stream_chunk, "dp", 2), axis=0)

    def in_order(near_half):
        stacked = near_half.reshape(planes, chunk, width)
        own_half = jnp.concatenate(
            [lax.dynamic_index_in_dim(stacked, plane ^ p, 0, keepdims=False) for p in range(planes)], axis=0
        )
        other = swap(own_half, "dp", 1)
        lower = jnp.where(core == 0, own_half, other)
        upper = jnp.where(core == 0, other, own_half)
        return jnp.concatenate([lower, upper], axis=0)

    move_cap = 2 * row_count // owners
    target = my_slots // row_count
    target_hot = (target[:, None] == jnp.arange(owners)[None, :]).astype(jnp.int32)
    earlier = jnp.sum((jnp.cumsum(target_hot, axis=0) - target_hot) * target_hot, axis=1)
    send_slot = (target ^ own) * move_cap + earlier
    slot_count = owners * move_cap
    send_hot = (jnp.arange(slot_count)[:, None] == send_slot[None, :]).astype(BF16)
    moving = jnp.concatenate([ssm_old, conv_state[:, 1:, :]], axis=1).reshape(row_count, -1)
    packed = (
        jnp.dot(send_hot, moving, preferred_element_type=F32).astype(BF16).reshape(owners, move_cap, -1)
    )
    arrived = jnp.concatenate(
        [packed[0]] + [swap(packed[flip], "expert", flip) for flip in range(1, owners)], axis=0
    )
    arriving = (new_slot // row_count == own).astype(jnp.int32).reshape(owners, row_count)
    arrive_rank = (jnp.cumsum(arriving, axis=1) - arriving).reshape(-1)
    source_ids = jnp.arange(rows) // row_count
    recv_slot = (source_ids ^ own) * move_cap + arrive_rank
    place_rows = (
        (new_slot[None, :] == (own * row_count + jnp.arange(row_count))[:, None])
    ).astype(BF16)
    place_slots = (recv_slot[:, None] == jnp.arange(slot_count)[None, :]).astype(BF16)
    place_hot = jnp.dot(place_rows, place_slots, preferred_element_type=F32).astype(BF16)
    moved = (
        jnp.dot(place_hot, arrived, preferred_element_type=F32)
        .astype(BF16)
        .reshape(row_count, state_dim + tap_count - 2, channels)
    )
    ssm_new = moved[:, :state_dim]
    conv_new = jnp.concatenate([moved[:, state_dim:], conv_input[:, None, :]], axis=1)

    capacity = min(row_count, 5 * row_count * routes.shape[1] // (2 * owners))
    if capacity < row_count:
        layer_out = dispatch_experts(
            in_order(stream_half),
            norm_gain,
            routes,
            gate_weight,
            expert_gate[0],
            expert_up[0],
            expert_down[0],
            row_count,
            capacity,
        )
        return (ssm_new, conv_new, layer_out)

    blocks = gather_pairs(stream_half, "expert")
    blocks = [jnp.concatenate([block, swap(block, "dp", 1)], axis=0).astype(F32) for block in blocks]
    square = sum(jnp.sum(block * block, axis=1, keepdims=True) for block in blocks)
    scale = lax.rsqrt(square / (owners * width) + 1e-05)
    gains = norm_gain.reshape(owners, 1, width)
    near_normed = jnp.stack(
        [
            (block * scale * lax.dynamic_index_in_dim(gains, own ^ flip, 0, keepdims=False)).astype(BF16)
            for flip, block in enumerate(blocks)
        ]
    )
    normed = jnp.concatenate(
        [lax.dynamic_index_in_dim(near_normed, own ^ e, 0, keepdims=False) for e in range(owners)], axis=1
    )
    gate_val = jnp.dot(normed, expert_gate[0], preferred_element_type=F32)
    up_val = jnp.dot(normed, expert_up[0], preferred_element_type=F32)
    hidden = (jax.nn.silu(gate_val) * up_val).astype(BF16)
    near_rows = (
        (jnp.arange(2) ^ core)[:, None, None] * half
        + (jnp.arange(planes) ^ plane)[None, :, None] * chunk
        + jnp.arange(chunk)[None, None, :]
    ).reshape(-1)
    row_weight = jnp.sum(jnp.where(routes == own, gate_weight, 0.0), axis=1)
    near_weight = jnp.sum(
        jnp.where(near_rows[:, None] == jnp.arange(rows)[None, :], row_weight[None, :], 0.0), axis=1, keepdims=True
    )
    expert_out = (jnp.dot(hidden, expert_down[0], preferred_element_type=F32) * near_weight).astype(BF16)

    out_half = expert_out[:half].astype(F32) + swap(expert_out[half:], "dp", 1).astype(F32)
    own_columns = scatter_pairs(
        [lax.dynamic_slice_in_dim(out_half, (own ^ flip) * width, width, axis=1) for flip in range(owners)], "expert"
    ).reshape(planes, chunk, width)
    mix_rows = scatter_pairs([own_columns[flip] for flip in range(planes)], "dp", 2)
    layer_chunk = (stream_chunk.astype(F32) + mix_rows).astype(BF16)
    layer_out = in_order(jnp.concatenate(gather_pairs(layer_chunk, "dp", 2), axis=0))
    return (ssm_new, conv_new, layer_out)


def solution(mesh):
    in_specs = (
        P("expert", None, "dp"),
        P("expert", None, "dp"),
        P(),
        P("expert", "dp"),
        P("expert", "dp"),
        P(None, "dp"),
        P("dp"),
        P("dp", None),
        P(None, "dp"),
        P("dp"),
        P(None, "dp"),
        P("dp"),
        P("dp", "expert"),
        P(None, "expert"),
        P(),
        P(),
        P(),
        P("expert", None, "dp"),
        P("expert", None, "dp"),
        P("expert", "dp", None),
    )
    out_specs = (P("expert", None, "dp"), P("expert", None, "dp"), P(None, "expert"))
    return jax.shard_map(body, mesh=mesh, in_specs=in_specs, out_specs=out_specs, check_vma=False)
```

```python
import jax
import jax.numpy as jnp
from jax import lax
from jax.experimental import pallas as pl
from jax.experimental.pallas import tpu as pltpu
from jax.sharding import PartitionSpec as P

F32 = jnp.float32
BF16 = jnp.bfloat16


def swap(values, axis, flip):
    size = lax.axis_size(axis)
    return lax.ppermute(values, axis, [(i, i ^ flip) for i in range(size)])


def gather_pairs(values, axis, stride=1):
    count = lax.axis_size(axis) // stride
    return [values] + [swap(values, axis, flip * stride) for flip in range(1, count)]


def scatter_pairs(parts, axis, stride=1):
    total = parts[0].astype(F32)
    for flip in range(1, len(parts)):
        total = total + swap(parts[flip].astype(BF16), axis, flip * stride).astype(F32)
    return total


def dispatch_experts(stream, norm_gain, routes, gate_weight, expert_gate, expert_up, expert_down, row_count, capacity):
    owners = lax.axis_size("expert")
    top_count = routes.shape[1]
    width = stream.shape[1]
    expert_hot = (
        (routes[:, :, None] == jnp.arange(owners)[None, None, :])
        .astype(jnp.int32)
        .reshape(owners, row_count * top_count, owners)
    )
    prior = jnp.sum((jnp.cumsum(expert_hot, axis=1) - expert_hot) * expert_hot, axis=2)
    slot_of = (routes.reshape(owners, row_count * top_count) * capacity + prior).reshape(owners, row_count, top_count)
    matches = slot_of[:, :, :, None] == jnp.arange(owners * capacity)[None, None, None, :]
    dispatch_hot = jnp.any(matches, axis=2).astype(BF16).reshape(owners, row_count, owners, capacity)
    combine_w = jnp.sum(
        jnp.where(matches, gate_weight.reshape(owners, row_count, top_count)[:, :, :, None], 0.0), axis=2
    ).reshape(owners, row_count, owners, capacity)
    outgoing = jnp.einsum(
        "orec,ord->eocd", dispatch_hot, stream.reshape(owners, row_count, width), preferred_element_type=F32
    ).astype(BF16)
    arrived = lax.all_to_all(outgoing, "expert", split_axis=0, concat_axis=3, tiled=True)
    tokens = arrived.reshape(owners * capacity, -1).astype(F32)
    normed = (
        tokens * lax.rsqrt(jnp.mean(tokens * tokens, axis=1, keepdims=True) + 1e-05) * norm_gain[None, :]
    ).astype(BF16)
    gate_val = jnp.dot(normed, expert_gate, preferred_element_type=F32)
    up_val = jnp.dot(normed, expert_up, preferred_element_type=F32)
    hidden = (jax.nn.silu(gate_val) * up_val).astype(BF16)
    partial_out = jnp.dot(hidden, expert_down, preferred_element_type=F32).reshape(owners, capacity, -1)
    summed = lax.psum(partial_out, "dp")
    returned = lax.all_to_all(summed.astype(BF16), "expert", split_axis=2, concat_axis=0, tiled=True).astype(F32)
    expert_mix = jnp.einsum(
        "orec,eocd->ord",
        combine_w,
        returned.reshape(owners, owners, capacity, width),
        precision=lax.Precision.HIGHEST,
        preferred_element_type=F32,
    )
    return (stream.astype(F32) + expert_mix.reshape(-1, width)).astype(BF16)


def pack_rows(source_rows, states, segments):
    tails = [tail for _, _, tail in segments if tail is not None]
    extra = tails[0].shape[0]

    def kernel(rows_ref, states_ref, *refs):
        tail_refs, out_refs = list(refs[: len(tails)]), refs[len(tails) :]
        for (start, count, tail), out_ref in zip(segments, out_refs):

            def step(i, carry, start=start, out_ref=out_ref):
                out_ref[i] = states_ref[rows_ref[start + i]]
                return carry

            lax.fori_loop(0, count, step, 0, unroll=8)
            if tail is not None:
                out_ref[count:] = tail_refs.pop(0)[...]

    here = pl.BlockSpec(memory_space=pltpu.VMEM)
    return pl.pallas_call(
        kernel,
        out_shape=[
            jax.ShapeDtypeStruct((count + (0 if tail is None else extra),) + states.shape[1:], states.dtype)
            for _, count, tail in segments
        ],
        in_specs=[pl.BlockSpec(memory_space=pltpu.SMEM)] + [here] * (1 + len(tails)),
        out_specs=[here] * len(segments),
        name="pack_rows",
    )(source_rows, states, *tails)


def place_rows(source_rows, parts):
    counts = [part.shape[0] for part in parts]
    starts = [sum(counts[:k]) for k in range(len(parts))]
    row_shape = parts[0].shape[1:]
    row_count = source_rows.shape[0]

    def kernel(rows_ref, *refs):
        part_refs, (out_ref, held, sems) = refs[: len(parts)], refs[len(parts) :]
        copies = [
            pltpu.make_async_copy(part_ref, held.at[pl.ds(start, count)], sems.at[k])
            for k, (part_ref, start, count) in enumerate(zip(part_refs, starts, counts))
        ]
        for copy in copies:
            copy.start()
        for copy in copies:
            copy.wait()

        def step(i, carry):
            out_ref[i] = held[rows_ref[i]]
            return carry

        lax.fori_loop(0, row_count, step, 0, unroll=8)

    return pl.pallas_call(
        kernel,
        out_shape=jax.ShapeDtypeStruct((row_count,) + row_shape, parts[0].dtype),
        in_specs=[pl.BlockSpec(memory_space=pltpu.SMEM)] + [pl.BlockSpec(memory_space=pl.ANY)] * len(parts),
        out_specs=pl.BlockSpec(memory_space=pltpu.VMEM),
        scratch_shapes=[
            pltpu.VMEM((sum(counts),) + row_shape, parts[0].dtype),
            pltpu.SemaphoreType.DMA((len(parts),)),
        ],
        name="place_rows",
    )(source_rows, *parts)


def expert_kernel(owner_ids, blocks, gains, gate_w, up_w, carry=None, down=None):
    half, width = blocks[0][0].shape
    rows = 2 * half
    depth, hidden_dim = gate_w.shape
    count = len(blocks)
    tile = 256
    last = down is not None
    out_count = down[2] if last else 0

    def kernel(ids_ref, *refs):
        block_refs, refs = refs[: 2 * count], refs[2 * count :]
        gains_ref, gate_ref, up_ref = refs[:3]
        refs = list(refs[3:])
        if carry is not None:
            gate_in, up_in, square_in = (refs.pop(0) for _ in range(3))
            gate_carry, up_carry, carry_sems = (refs.pop() for _ in range(3))
        if last:
            down_ref, weight_ref = (refs.pop(0) for _ in range(2))
            out_refs = [refs.pop(0) for _ in range(2 * out_count)]
            hidden, down_buf, outs, tail_sems = (refs.pop() for _ in range(4))
        gate_sum, up_sum, square, mixed, gate_buf, up_buf, sems = refs

        def fetch(b, w):
            source, buf = ((gate_ref, gate_buf), (up_ref, up_buf))[w]
            at = pl.multiple_of(ids_ref[b] * width, width)
            return pltpu.make_async_copy(source.at[pl.ds(at, width)], buf.at[b], sems.at[b, w])

        def fetch_down(k):
            at = pl.multiple_of(ids_ref[count + k] * width, width)
            return pltpu.make_async_copy(down_ref.at[:, pl.ds(at, width)], down_buf.at[k], tail_sems.at[0, k])

        def fetch_carry(w):
            source, buf = ((gate_in, gate_carry), (up_in, up_carry))[w]
            return pltpu.make_async_copy(source, buf, carry_sems.at[w])

        def give(k, h):
            return pltpu.make_async_copy(outs.at[k, h], out_refs[2 * k + h], tail_sems.at[1 + h, k])

        queue = [[fetch(b, 0), fetch(b, 1)] for b in range(count)]
        if carry is not None:
            queue.append([fetch_carry(0), fetch_carry(1)])
        queue += [[fetch_down(k)] for k in range(out_count)]

        def start_next():
            if queue:
                for copy in queue.pop(0):
                    copy.start()

        start_next()
        start_next()
        square[...] = jnp.zeros_like(square) if carry is None else square_in[...]
        for b in range(count):
            gain = gains_ref[ids_ref[b]]
            for h in range(2):
                values = block_refs[2 * b + h][...].astype(F32)
                square[h * half : (h + 1) * half] += jnp.sum(values * values, axis=1, keepdims=True)
                mixed[b, h * half : (h + 1) * half] = (values * gain).astype(BF16)
        for b in range(count):
            fetch(b, 0).wait()
            fetch(b, 1).wait()
            start_next()
            if carry is not None and b == count - 1:
                fetch_carry(0).wait()
                fetch_carry(1).wait()
                start_next()
            if last and b == count - 1:
                scale = lax.rsqrt(square[...] / depth + 1e-05)
            left = mixed[b]
            for at in range(0, hidden_dim, tile):
                to = min(at + tile, hidden_dim)
                gate_val = jnp.dot(left, gate_buf[b, :, at:to], preferred_element_type=F32)
                up_val = jnp.dot(left, up_buf[b, :, at:to], preferred_element_type=F32)
                if b > 0:
                    gate_val, up_val = gate_val + gate_sum[:, at:to], up_val + up_sum[:, at:to]
                if carry is not None and b == count - 1:
                    gate_val, up_val = gate_val + gate_carry[:, at:to], up_val + up_carry[:, at:to]
                if last and b == count - 1:
                    hidden[:, at:to] = (jax.nn.silu(gate_val * scale) * (up_val * scale)).astype(BF16)
                else:
                    gate_sum[:, at:to] = gate_val
                    up_sum[:, at:to] = up_val
        for k in range(out_count):
            fetch_down(k).wait()
            start_next()
            for at in range(0, width, tile):
                out = jnp.dot(hidden[...], down_buf[k, :, at : at + tile], preferred_element_type=F32)
                out = out * weight_ref[...]
                outs[k, 0, :, at : at + tile] = out[:half].astype(BF16)
                outs[k, 1, :, at : at + tile] = out[half:].astype(BF16)
            give(k, 0).start()
            give(k, 1).start()
        for k in range(out_count):
            give(k, 0).wait()
            give(k, 1).wait()

    here = pl.BlockSpec(memory_space=pltpu.VMEM)
    anywhere = pl.BlockSpec(memory_space=pl.ANY)
    operands = [owner_ids] + [part for block in blocks for part in block] + [gains, gate_w, up_w]
    in_specs = [pl.BlockSpec(memory_space=pltpu.SMEM)] + [here] * (2 * count + 1) + [anywhere] * 2
    sums = [(rows, hidden_dim), (rows, hidden_dim), (rows, 1)]
    scratch = [
        pltpu.VMEM((count, rows, width), BF16),
        pltpu.VMEM((count, width, hidden_dim), BF16),
        pltpu.VMEM((count, width, hidden_dim), BF16),
        pltpu.SemaphoreType.DMA((count, 2)),
    ]
    if carry is not None:
        operands += list(carry)
        in_specs += [anywhere, anywhere, here]
    if last:
        operands += [down[0], down[1]]
        in_specs += [anywhere, here]
        out_shape = [jax.ShapeDtypeStruct((half, width), BF16)] * (2 * out_count)
        out_specs = [anywhere] * (2 * out_count)
        scratch = [pltpu.VMEM(shape, F32) for shape in sums] + scratch
        scratch += [
            pltpu.SemaphoreType.DMA((3, out_count)),
            pltpu.VMEM((out_count, 2, half, width), BF16),
            pltpu.VMEM((out_count, hidden_dim, width), BF16),
            pltpu.VMEM((rows, hidden_dim), BF16),
        ]
    else:
        out_shape = [jax.ShapeDtypeStruct(shape, F32) for shape in sums]
        out_specs = [here] * 3
    if carry is not None:
        scratch += [
            pltpu.SemaphoreType.DMA((2,)),
            pltpu.VMEM((rows, hidden_dim), F32),
            pltpu.VMEM((rows, hidden_dim), F32),
        ]
    return pl.pallas_call(
        kernel,
        out_shape=out_shape,
        in_specs=in_specs,
        out_specs=out_specs,
        scratch_shapes=scratch,
        compiler_params=pltpu.CompilerParams(vmem_limit_bytes=56 * 1024 * 1024),
        name="expert_outputs" if last else "expert_sums",
    )(*operands)


def body(
    ssm_state,
    conv_state,
    new_slot,
    conv_input,
    gate_input,
    conv_weight,
    conv_bias,
    x_proj_weight,
    step_weight,
    step_bias,
    decay_log,
    skip_gain,
    out_proj_weight,
    residual,
    norm_gain,
    routes,
    gate_weight,
    expert_gate,
    expert_up,
    expert_down,
):
    row_count, state_dim, channels = ssm_state.shape
    owners = lax.axis_size("expert")
    own = lax.axis_index("expert")
    dp_index = lax.axis_index("dp")
    core = dp_index % 2
    plane = dp_index // 2
    planes = lax.axis_size("dp") // 2
    rows = owners * row_count
    half = rows // 2
    chunk = half // planes
    tap_count = conv_weight.shape[0]

    conv_all = jnp.concatenate(gather_pairs(conv_input, "expert"), axis=0)
    my_slots = lax.dynamic_slice_in_dim(new_slot, own * row_count, row_count)
    near_ids = (
        (jnp.arange(owners) ^ own)[:, None] * row_count + jnp.arange(row_count)[None, :]
    ).reshape(-1)
    pick = (my_slots[:, None] == near_ids[None, :]).astype(BF16)
    conv_in = jnp.dot(pick, conv_all, preferred_element_type=F32)

    conv_sum = (
        jnp.sum(conv_state.astype(F32) * conv_weight[None, : tap_count - 1, :], axis=1)
        + conv_in * conv_weight[tap_count - 1][None, :]
        + conv_bias[None, :]
    )
    activated = jax.nn.silu(conv_sum).astype(BF16)
    projected = jnp.dot(activated, x_proj_weight, preferred_element_type=F32)
    projected = projected + swap(projected, "dp", 1)
    new_slot, my_slots, gate_input, projected = lax.optimization_barrier(
        (new_slot, my_slots, gate_input, projected)
    )
    gate_all = jnp.concatenate(gather_pairs(gate_input, "expert"), axis=0)
    projected = scatter_pairs([projected] * planes, "dp", 2)

    move_cap = 2 * row_count // owners
    slot_count = owners * move_cap
    target = my_slots // row_count
    target_hot = (target[:, None] == jnp.arange(owners)[None, :]).astype(jnp.int32)
    earlier = jnp.sum((jnp.cumsum(target_hot, axis=0) - target_hot) * target_hot, axis=1)
    send_slot = (target ^ own) * move_cap + earlier
    send_match = jnp.arange(slot_count)[:, None] == send_slot[None, :]
    send_rows = jnp.sum(jnp.where(send_match, jnp.arange(row_count)[None, :], 0), axis=1)
    conv_keep = conv_state[:, 1:, :]
    conv_moving = jnp.dot(
        send_match.astype(BF16), conv_keep.reshape(row_count, -1), preferred_element_type=F32
    ).astype(BF16)
    tails = conv_moving.reshape(owners, -1, state_dim, channels)
    tail_rows = tails.shape[1]
    arriving = (new_slot // row_count == own).astype(jnp.int32).reshape(owners, row_count)
    arrive_rank = (jnp.cumsum(arriving, axis=1) - arriving).reshape(-1)
    source_flip = (jnp.arange(rows) // row_count) ^ own
    from_here = source_flip == 0
    here_row = jnp.arange(rows) % row_count
    is_source = new_slot[None, :] == (own * row_count + jnp.arange(row_count))[:, None]

    early = owners // 2

    def source_of(extra):
        at = row_count + (source_flip - 1) * (move_cap + extra) + arrive_rank
        return jnp.sum(jnp.where(is_source, jnp.where(from_here, here_row, at)[None, :], 0), axis=1)

    ssm_source = source_of(tail_rows)
    conv_source = source_of(0)

    rank_dim = step_weight.shape[0]
    step_low = projected[:, :rank_dim]
    b_coef = projected[:, rank_dim : rank_dim + state_dim]
    c_coef = projected[:, rank_dim + state_dim :]
    step_norm = (
        step_low * lax.rsqrt(jnp.mean(step_low * step_low, axis=1, keepdims=True) + 1e-06)
    ).astype(BF16)
    step_size = jax.nn.softplus(
        jnp.dot(step_norm, step_weight, preferred_element_type=F32) + step_bias[None, :]
    )
    act_float = activated.astype(F32)

    def update(state, step, rate, b_in):
        decays = jnp.exp(step[:, None, :] * rate[None, :, :])
        return decays * state.astype(F32) + (step * act_float)[:, None, :] * b_in[:, :, None]

    rate = -jnp.exp(decay_log)
    states = update(ssm_state, step_size, rate, b_coef)
    gate_in = jnp.dot(pick, gate_all, preferred_element_type=F32)
    gated_out = (
        (jnp.sum(c_coef[:, :, None] * states, axis=1) + skip_gain[None, :] * act_float) * jax.nn.silu(gate_in)
    ).astype(BF16)
    gated_out, *again = lax.optimization_barrier((gated_out, ssm_state, step_size, rate, b_coef))
    ssm_old = update(*again).astype(BF16)

    near_rows = (
        (jnp.arange(2) ^ core)[:, None, None] * half
        + (jnp.arange(planes) ^ plane)[None, :, None] * chunk
        + jnp.arange(chunk)[None, None, :]
    ).reshape(-1)
    gated_all = jnp.concatenate(gather_pairs(gated_out, "expert"), axis=0)
    packed = pack_rows(
        send_rows, ssm_old, [(flip * move_cap, move_cap, tails[flip]) for flip in range(1, owners)]
    )
    gated_all, *packed = lax.optimization_barrier((gated_all, *packed))
    old_slots = new_slot.reshape(owners, row_count)
    near_slots = jnp.concatenate(
        [lax.dynamic_slice_in_dim(old_slots, own ^ flip, 1, axis=0) for flip in range(owners)], axis=0
    ).reshape(-1)
    order_hot = (near_rows[:, None] == near_slots[None, :]).astype(BF16)
    gated_new = jnp.dot(order_hot, gated_all, preferred_element_type=F32).astype(BF16)
    mix = jnp.dot(gated_new, out_proj_weight, preferred_element_type=F32)
    width = mix.shape[1]

    now = [swap(part, "expert", flip) for flip, part in enumerate(packed[:early], 1)]

    mix_half = mix[:half] + swap(mix[half:].astype(BF16), "dp", 1).astype(F32)
    gate_w, up_w, down_w = expert_gate[0], expert_up[0], expert_down[0]
    capacity = min(row_count, 5 * row_count * routes.shape[1] // (2 * owners))
    dense = capacity == row_count
    mix_chunk = scatter_pairs(list(mix_half.reshape(planes, chunk, width)), "dp", 2)
    residual_chunk = lax.dynamic_slice_in_dim(residual, core * half + plane * chunk, chunk, axis=0)
    stream_chunk = (residual_chunk.astype(F32) + mix_chunk).astype(BF16)
    stream_half = jnp.concatenate(gather_pairs(stream_chunk, "dp", 2), axis=0)
    stream_half, *now = lax.optimization_barrier((stream_half, *now))

    def in_order(near_half):
        stacked = near_half.reshape(planes, chunk, width)
        own_half = jnp.concatenate(
            [lax.dynamic_index_in_dim(stacked, plane ^ p, 0, keepdims=False) for p in range(planes)], axis=0
        )
        other = swap(own_half, "dp", 1)
        return jnp.where(
            core == 0, jnp.concatenate([own_half, other], axis=0), jnp.concatenate([other, own_half], axis=0)
        )

    def finish_states(later):
        ssm_new = place_rows(ssm_source, [ssm_old] + now + later)
        conv_rows = [conv_keep.reshape(row_count, -1)] + [
            part[-tail_rows:].reshape(move_cap, -1) for part in now + later
        ]
        conv_rows = jnp.concatenate(conv_rows, axis=0)
        conv_hot = (conv_source[:, None] == jnp.arange(conv_rows.shape[0])[None, :]).astype(BF16)
        conv_moved = jnp.dot(conv_hot, conv_rows, preferred_element_type=F32).astype(BF16)
        conv_new = jnp.concatenate(
            [conv_moved.reshape(row_count, tap_count - 2, channels), conv_input[:, None, :]], axis=1
        )
        return ssm_new, conv_new

    if not dense:
        later = [swap(part, "expert", flip) for flip, part in enumerate(packed[early:], early + 1)]
        stream = in_order(stream_half)
        layer_out = dispatch_experts(
            stream,
            norm_gain,
            routes,
            gate_weight,
            gate_w,
            up_w,
            down_w,
            row_count,
            capacity,
        )
        return (*finish_states(later), layer_out)

    blocks = gather_pairs(stream_half, "expert")
    gains = norm_gain.reshape(owners, 1, width)
    near_owners = jnp.arange(owners, dtype=jnp.int32) ^ own
    row_weight = jnp.sum(jnp.where(routes == own, gate_weight, 0.0), axis=1)
    near_weight = jnp.sum(
        jnp.where(near_rows[:, None] == jnp.arange(rows)[None, :], row_weight[None, :], 0.0), axis=1, keepdims=True
    )
    near_weight, blocks[0] = lax.optimization_barrier((near_weight, blocks[0]))
    pairs = [(block, swap(block, "dp", 1)) for block in blocks[:early]]
    sums = expert_kernel(near_owners[:early], pairs, gains, gate_w, up_w)
    last_count = owners - early
    tied = lax.optimization_barrier((*blocks[early:], *packed[early:], *sums))
    pairs = [(block, swap(block, "dp", 1)) for block in tied[:last_count]]
    later = [swap(part, "expert", flip) for flip, part in enumerate(tied[last_count:-3], early + 1)]
    outs = expert_kernel(
        jnp.concatenate([near_owners[early:], near_owners]),
        pairs,
        gains,
        gate_w,
        up_w,
        tied[-3:],
        (down_w, near_weight, owners),
    )

    others = [swap(outs[2 * k + 1], "dp", 1) for k in range(owners)]
    tied = lax.optimization_barrier((*others, *later))
    others, later = tied[:owners], list(tied[owners:])
    own_columns = scatter_pairs(
        [(outs[2 * k].astype(F32) + others[k].astype(F32)).astype(BF16) for k in range(owners)], "expert"
    )
    own_columns, *done = lax.optimization_barrier((own_columns, *finish_states(later)))

    mix_rows = scatter_pairs(list(own_columns.reshape(planes, chunk, width)), "dp", 2)
    layer_chunk = (stream_chunk.astype(F32) + mix_rows).astype(BF16)
    layer_half = jnp.concatenate(gather_pairs(layer_chunk, "dp", 2), axis=0)
    return (*done, in_order(layer_half))


def solution(mesh):
    in_specs = (
        P("expert", None, "dp"),
        P("expert", None, "dp"),
        P(),
        P("expert", "dp"),
        P("expert", "dp"),
        P(None, "dp"),
        P("dp"),
        P("dp", None),
        P(None, "dp"),
        P("dp"),
        P(None, "dp"),
        P("dp"),
        P("dp", "expert"),
        P(None, "expert"),
        P(),
        P(),
        P(),
        P("expert", None, "dp"),
        P("expert", None, "dp"),
        P("expert", "dp", None),
    )
    out_specs = (P("expert", None, "dp"), P("expert", None, "dp"), P(None, "expert"))
    return jax.shard_map(body, mesh=mesh, in_specs=in_specs, out_specs=out_specs, check_vma=False)
```

```python
import jax
import jax.numpy as jnp
from jax import lax
from jax.experimental import pallas as pl
from jax.experimental.pallas import tpu as pltpu
from jax.sharding import PartitionSpec as P

F32 = jnp.float32
BF16 = jnp.bfloat16


def swap(values, axis, flip):
    size = lax.axis_size(axis)
    return lax.ppermute(values, axis, [(i, i ^ flip) for i in range(size)])


def gather_pairs(values, axis, stride=1):
    count = lax.axis_size(axis) // stride
    return [values] + [swap(values, axis, flip * stride) for flip in range(1, count)]


def scatter_pairs(parts, axis, stride=1):
    total = parts[0].astype(F32)
    for flip in range(1, len(parts)):
        total = total + swap(parts[flip].astype(BF16), axis, flip * stride).astype(F32)
    return total


def dispatch_experts(stream, norm_gain, routes, gate_weight, expert_gate, expert_up, expert_down, row_count, capacity):
    owners = lax.axis_size("expert")
    top_count = routes.shape[1]
    width = stream.shape[1]
    expert_hot = (
        (routes[:, :, None] == jnp.arange(owners)[None, None, :])
        .astype(jnp.int32)
        .reshape(owners, row_count * top_count, owners)
    )
    prior = jnp.sum((jnp.cumsum(expert_hot, axis=1) - expert_hot) * expert_hot, axis=2)
    slot_of = (routes.reshape(owners, row_count * top_count) * capacity + prior).reshape(owners, row_count, top_count)
    matches = slot_of[:, :, :, None] == jnp.arange(owners * capacity)[None, None, None, :]
    dispatch_hot = jnp.any(matches, axis=2).astype(BF16).reshape(owners, row_count, owners, capacity)
    combine_w = jnp.sum(
        jnp.where(matches, gate_weight.reshape(owners, row_count, top_count)[:, :, :, None], 0.0), axis=2
    ).reshape(owners, row_count, owners, capacity)
    outgoing = jnp.einsum(
        "orec,ord->eocd", dispatch_hot, stream.reshape(owners, row_count, width), preferred_element_type=F32
    ).astype(BF16)
    arrived = lax.all_to_all(outgoing, "expert", split_axis=0, concat_axis=3, tiled=True)
    tokens = arrived.reshape(owners * capacity, -1).astype(F32)
    normed = (
        tokens * lax.rsqrt(jnp.mean(tokens * tokens, axis=1, keepdims=True) + 1e-05) * norm_gain[None, :]
    ).astype(BF16)
    gate_val = jnp.dot(normed, expert_gate, preferred_element_type=F32)
    up_val = jnp.dot(normed, expert_up, preferred_element_type=F32)
    hidden = (jax.nn.silu(gate_val) * up_val).astype(BF16)
    partial_out = jnp.dot(hidden, expert_down, preferred_element_type=F32).reshape(owners, capacity, -1)
    summed = lax.psum(partial_out, "dp")
    returned = lax.all_to_all(summed.astype(BF16), "expert", split_axis=2, concat_axis=0, tiled=True).astype(F32)
    expert_mix = jnp.einsum(
        "orec,eocd->ord",
        combine_w,
        returned.reshape(owners, owners, capacity, width),
        precision=lax.Precision.HIGHEST,
        preferred_element_type=F32,
    )
    return (stream.astype(F32) + expert_mix.reshape(-1, width)).astype(BF16)


def pack_rows(source_rows, states, segments):
    tails = [tail for _, _, tail in segments if tail is not None]
    extra = tails[0].shape[0]

    def kernel(rows_ref, states_ref, *refs):
        tail_refs, out_refs = list(refs[: len(tails)]), refs[len(tails) :]
        for (start, count, tail), out_ref in zip(segments, out_refs):

            def step(i, carry, start=start, out_ref=out_ref):
                out_ref[i] = states_ref[rows_ref[start + i]]
                return carry

            lax.fori_loop(0, count, step, 0, unroll=8)
            if tail is not None:
                out_ref[count:] = tail_refs.pop(0)[...]

    here = pl.BlockSpec(memory_space=pltpu.VMEM)
    return pl.pallas_call(
        kernel,
        out_shape=[
            jax.ShapeDtypeStruct((count + (0 if tail is None else extra),) + states.shape[1:], states.dtype)
            for _, count, tail in segments
        ],
        in_specs=[pl.BlockSpec(memory_space=pltpu.SMEM)] + [here] * (1 + len(tails)),
        out_specs=[here] * len(segments),
        name="pack_rows",
    )(source_rows, states, *tails)


def place_rows(source_rows, parts):
    counts = [part.shape[0] for part in parts]
    starts = [sum(counts[:k]) for k in range(len(parts))]
    row_shape = parts[0].shape[1:]
    row_count = source_rows.shape[0]

    def kernel(rows_ref, *refs):
        part_refs, (out_ref, held, sems) = refs[: len(parts)], refs[len(parts) :]
        copies = [
            pltpu.make_async_copy(part_ref, held.at[pl.ds(start, count)], sems.at[k])
            for k, (part_ref, start, count) in enumerate(zip(part_refs, starts, counts))
        ]
        for copy in copies:
            copy.start()
        for copy in copies:
            copy.wait()

        def step(i, carry):
            out_ref[i] = held[rows_ref[i]]
            return carry

        lax.fori_loop(0, row_count, step, 0, unroll=8)

    return pl.pallas_call(
        kernel,
        out_shape=jax.ShapeDtypeStruct((row_count,) + row_shape, parts[0].dtype),
        in_specs=[pl.BlockSpec(memory_space=pltpu.SMEM)] + [pl.BlockSpec(memory_space=pl.ANY)] * len(parts),
        out_specs=pl.BlockSpec(memory_space=pltpu.VMEM),
        scratch_shapes=[
            pltpu.VMEM((sum(counts),) + row_shape, parts[0].dtype),
            pltpu.SemaphoreType.DMA((len(parts),)),
        ],
        name="place_rows",
    )(source_rows, *parts)


def expert_kernel(owner_ids, first, blocks, gains, gate_w, up_w, row_weight, carry=None, down_w=None):
    half, width = blocks[0][0].shape
    rows = 2 * half
    depth, hidden_dim = gate_w.shape
    count = len(blocks)
    tile = 256
    last = down_w is not None
    out_count = owner_ids.shape[0] if last else 0

    def kernel(ids_ref, *refs):
        block_refs, refs = refs[: 2 * count], refs[2 * count :]
        gains_ref, gate_ref, up_ref, weight_ref = refs[:4]
        refs = list(refs[4:])
        if carry is not None:
            gate_in, up_in, square_in = (refs.pop(0) for _ in range(3))
            gate_carry, up_carry, carry_sems = (refs.pop() for _ in range(3))
        if last:
            down_ref = refs.pop(0)
            out_refs = [refs.pop(0) for _ in range(2 * out_count)]
            hidden, down_buf, outs, tail_sems = (refs.pop() for _ in range(4))
        gate_sum, up_sum, square, raw, raw_sems, mixed, gate_buf, up_buf, sems = refs

        def fetch_block(b, h):
            return pltpu.make_async_copy(block_refs[2 * b + h], raw.at[b, h], raw_sems.at[b, h])

        def fetch(b, w):
            source, buf = ((gate_ref, gate_buf), (up_ref, up_buf))[w]
            at = pl.multiple_of(ids_ref[first + b] * width, width)
            return pltpu.make_async_copy(source.at[pl.ds(at, width)], buf.at[b], sems.at[b, w])

        def fetch_down(k):
            at = pl.multiple_of(ids_ref[k] * width, width)
            return pltpu.make_async_copy(down_ref.at[:, pl.ds(at, width)], down_buf.at[k], tail_sems.at[0, k])

        def fetch_carry(w):
            source, buf = ((gate_in, gate_carry), (up_in, up_carry))[w]
            return pltpu.make_async_copy(source, buf, carry_sems.at[w])

        def give(k, h):
            return pltpu.make_async_copy(outs.at[k, h], out_refs[2 * k + h], tail_sems.at[1 + h, k])

        queue = [[fetch(b, 0), fetch(b, 1)] for b in range(count)]
        if carry is not None:
            queue.append([fetch_carry(0), fetch_carry(1)])
        queue += [[fetch_down(k)] for k in range(out_count)]

        for b in range(count):
            fetch_block(b, 0).start()
            fetch_block(b, 1).start()

        def start_next():
            if queue:
                for copy in queue.pop(0):
                    copy.start()

        start_next()
        start_next()
        square[...] = jnp.zeros_like(square) if carry is None else square_in[...]
        for b in range(count):
            gain = gains_ref[ids_ref[first + b]]
            for h in range(2):
                fetch_block(b, h).wait()
                values = raw[b, h].astype(F32)
                square[h * half : (h + 1) * half] += jnp.sum(values * values, axis=1, keepdims=True)
                mixed[b, h * half : (h + 1) * half] = (values * gain).astype(BF16)
        for b in range(count):
            fetch(b, 0).wait()
            fetch(b, 1).wait()
            start_next()
            if carry is not None and b == count - 1:
                fetch_carry(0).wait()
                fetch_carry(1).wait()
                start_next()
            if last and b == count - 1:
                scale = lax.rsqrt(square[...] / depth + 1e-05)
            left = mixed[b]
            for at in range(0, hidden_dim, tile):
                to = min(at + tile, hidden_dim)
                gate_val = jnp.dot(left, gate_buf[b, :, at:to], preferred_element_type=F32)
                up_val = jnp.dot(left, up_buf[b, :, at:to], preferred_element_type=F32)
                if b > 0:
                    gate_val, up_val = gate_val + gate_sum[:, at:to], up_val + up_sum[:, at:to]
                if carry is not None and b == count - 1:
                    gate_val, up_val = gate_val + gate_carry[:, at:to], up_val + up_carry[:, at:to]
                if last and b == count - 1:
                    hidden[:, at:to] = (jax.nn.silu(gate_val * scale) * (up_val * scale)).astype(BF16)
                else:
                    gate_sum[:, at:to] = gate_val
                    up_sum[:, at:to] = up_val
        for k in range(out_count):
            fetch_down(k).wait()
            start_next()
            for at in range(0, width, tile):
                out = jnp.dot(hidden[...], down_buf[k, :, at : at + tile], preferred_element_type=F32)
                out = out * weight_ref[...]
                outs[k, 0, :, at : at + tile] = out[:half].astype(BF16)
                outs[k, 1, :, at : at + tile] = out[half:].astype(BF16)
            give(k, 0).start()
            give(k, 1).start()
        for k in range(out_count):
            give(k, 0).wait()
            give(k, 1).wait()

    here = pl.BlockSpec(memory_space=pltpu.VMEM)
    anywhere = pl.BlockSpec(memory_space=pl.ANY)
    operands = [owner_ids] + [part for block in blocks for part in block] + [gains, gate_w, up_w, row_weight]
    in_specs = [pl.BlockSpec(memory_space=pltpu.SMEM)] + [anywhere] * (2 * count) + [here, anywhere, anywhere, here]
    sums = [(rows, hidden_dim), (rows, hidden_dim), (rows, 1)]
    scratch = [
        pltpu.VMEM((count, 2, half, width), BF16),
        pltpu.SemaphoreType.DMA((count, 2)),
        pltpu.VMEM((count, rows, width), BF16),
        pltpu.VMEM((count, width, hidden_dim), BF16),
        pltpu.VMEM((count, width, hidden_dim), BF16),
        pltpu.SemaphoreType.DMA((count, 2)),
    ]
    if carry is not None:
        operands += list(carry)
        in_specs += [anywhere, anywhere, here]
    if last:
        operands += [down_w]
        in_specs += [anywhere]
        out_shape = [jax.ShapeDtypeStruct((half, width), BF16)] * (2 * out_count)
        out_specs = [anywhere] * (2 * out_count)
        scratch = [pltpu.VMEM(shape, F32) for shape in sums] + scratch
        scratch += [
            pltpu.SemaphoreType.DMA((3, out_count)),
            pltpu.VMEM((out_count, 2, half, width), BF16),
            pltpu.VMEM((out_count, hidden_dim, width), BF16),
            pltpu.VMEM((rows, hidden_dim), BF16),
        ]
    else:
        out_shape = [jax.ShapeDtypeStruct(shape, F32) for shape in sums]
        out_specs = [here] * 3
    if carry is not None:
        scratch += [
            pltpu.SemaphoreType.DMA((2,)),
            pltpu.VMEM((rows, hidden_dim), F32),
            pltpu.VMEM((rows, hidden_dim), F32),
        ]
    return pl.pallas_call(
        kernel,
        out_shape=out_shape,
        in_specs=in_specs,
        out_specs=out_specs,
        scratch_shapes=scratch,
        compiler_params=pltpu.CompilerParams(vmem_limit_bytes=56 * 1024 * 1024),
        name="expert_outputs" if last else "expert_sums",
    )(*operands)


def add_pairs(lefts, rights, cut):
    count = len(lefts)
    rows, width = lefts[0].shape

    def kernel(*refs):
        left_refs, right_refs, out_refs = refs[:count], refs[count : 2 * count], refs[2 * count : 4 * count]
        held, sums, in_sems, out_sems = refs[4 * count :]

        def take(k, w):
            return pltpu.make_async_copy((left_refs, right_refs)[w][k], held.at[k, w], in_sems.at[k, w])

        def give(k, w):
            part = sums.at[k, pl.ds(w * cut, rows - cut if w else cut)]
            return pltpu.make_async_copy(part, out_refs[2 * k + w], out_sems.at[k, w])

        order = range(count - 1, -1, -1)
        for k in order:
            take(k, 0).start()
            take(k, 1).start()
        for k in order:
            take(k, 0).wait()
            take(k, 1).wait()
            sums[k] = (held[k, 0].astype(F32) + held[k, 1].astype(F32)).astype(BF16)
            give(k, 0).start()
            give(k, 1).start()
        for k in order:
            give(k, 0).wait()
            give(k, 1).wait()

    anywhere = pl.BlockSpec(memory_space=pl.ANY)
    return pl.pallas_call(
        kernel,
        out_shape=[jax.ShapeDtypeStruct((size, width), BF16) for _ in lefts for size in (cut, rows - cut)],
        in_specs=[anywhere] * (2 * count),
        out_specs=[anywhere] * (2 * count),
        scratch_shapes=[
            pltpu.VMEM((count, 2, rows, width), BF16),
            pltpu.VMEM((count, rows, width), BF16),
            pltpu.SemaphoreType.DMA((count, 2)),
            pltpu.SemaphoreType.DMA((count, 2)),
        ],
        name="add_pairs",
    )(*lefts, *rights)


def body(
    ssm_state,
    conv_state,
    new_slot,
    conv_input,
    gate_input,
    conv_weight,
    conv_bias,
    x_proj_weight,
    step_weight,
    step_bias,
    decay_log,
    skip_gain,
    out_proj_weight,
    residual,
    norm_gain,
    routes,
    gate_weight,
    expert_gate,
    expert_up,
    expert_down,
):
    row_count, state_dim, channels = ssm_state.shape
    owners = lax.axis_size("expert")
    own = lax.axis_index("expert")
    dp_index = lax.axis_index("dp")
    core = dp_index % 2
    plane = dp_index // 2
    planes = lax.axis_size("dp") // 2
    rows = owners * row_count
    half = rows // 2
    chunk = half // planes
    tap_count = conv_weight.shape[0]

    last = swap(jnp.concatenate([conv_input, gate_input], axis=0), "expert", owners - 1)
    conv_all = jnp.concatenate(
        [conv_input] + [swap(conv_input, "expert", flip) for flip in range(1, owners - 1)] + [last[:row_count]], axis=0
    )
    my_slots = lax.dynamic_slice_in_dim(new_slot, own * row_count, row_count)
    near_ids = (
        (jnp.arange(owners) ^ own)[:, None] * row_count + jnp.arange(row_count)[None, :]
    ).reshape(-1)
    pick = (my_slots[:, None] == near_ids[None, :]).astype(BF16)
    conv_in = jnp.dot(pick, conv_all, preferred_element_type=F32)

    conv_sum = (
        jnp.sum(conv_state.astype(F32) * conv_weight[None, : tap_count - 1, :], axis=1)
        + conv_in * conv_weight[tap_count - 1][None, :]
        + conv_bias[None, :]
    )
    activated = jax.nn.silu(conv_sum).astype(BF16)
    projected = jnp.dot(activated, x_proj_weight, preferred_element_type=F32)
    projected = projected + swap(projected, "dp", 1)
    new_slot, my_slots, gate_input, projected = lax.optimization_barrier(
        (new_slot, my_slots, gate_input, projected)
    )
    gate_all = jnp.concatenate(
        [gate_input] + [swap(gate_input, "expert", flip) for flip in range(1, owners - 1)] + [last[row_count:]], axis=0
    )
    projected = scatter_pairs([projected] * planes, "dp", 2)

    move_cap = 2 * row_count // owners
    slot_count = owners * move_cap
    target = my_slots // row_count
    target_hot = (target[:, None] == jnp.arange(owners)[None, :]).astype(jnp.int32)
    earlier = jnp.sum((jnp.cumsum(target_hot, axis=0) - target_hot) * target_hot, axis=1)
    send_slot = (target ^ own) * move_cap + earlier
    send_match = jnp.arange(slot_count)[:, None] == send_slot[None, :]
    send_rows = jnp.sum(jnp.where(send_match, jnp.arange(row_count)[None, :], 0), axis=1)
    conv_keep = conv_state[:, 1:, :]
    conv_moving = jnp.dot(
        send_match.astype(BF16), conv_keep.reshape(row_count, -1), preferred_element_type=F32
    ).astype(BF16)
    tails = conv_moving.reshape(owners, -1, state_dim, channels)
    tail_rows = tails.shape[1]
    arriving = (new_slot // row_count == own).astype(jnp.int32).reshape(owners, row_count)
    arrive_rank = (jnp.cumsum(arriving, axis=1) - arriving).reshape(-1)
    source_flip = (jnp.arange(rows) // row_count) ^ own
    from_here = source_flip == 0
    here_row = jnp.arange(rows) % row_count
    is_source = new_slot[None, :] == (own * row_count + jnp.arange(row_count))[:, None]

    early = owners // 2

    def source_of(extra):
        at = row_count + (source_flip - 1) * (move_cap + extra) + arrive_rank
        return jnp.sum(jnp.where(is_source, jnp.where(from_here, here_row, at)[None, :], 0), axis=1)

    ssm_source = source_of(tail_rows)
    conv_source = source_of(0)

    rank_dim = step_weight.shape[0]
    step_low = projected[:, :rank_dim]
    b_coef = projected[:, rank_dim : rank_dim + state_dim]
    c_coef = projected[:, rank_dim + state_dim :]
    step_norm = (
        step_low * lax.rsqrt(jnp.mean(step_low * step_low, axis=1, keepdims=True) + 1e-06)
    ).astype(BF16)
    step_size = jax.nn.softplus(
        jnp.dot(step_norm, step_weight, preferred_element_type=F32) + step_bias[None, :]
    )
    act_float = activated.astype(F32)

    def update(state, step, rate, b_in):
        decays = jnp.exp(step[:, None, :] * rate[None, :, :])
        return decays * state.astype(F32) + (step * act_float)[:, None, :] * b_in[:, :, None]

    rate = -jnp.exp(decay_log)
    states = update(ssm_state, step_size, rate, b_coef)
    gate_in = jnp.dot(pick, gate_all, preferred_element_type=F32)
    gated_out = (
        (jnp.sum(c_coef[:, :, None] * states, axis=1) + skip_gain[None, :] * act_float) * jax.nn.silu(gate_in)
    ).astype(BF16)
    gated_out, *again = lax.optimization_barrier((gated_out, ssm_state, step_size, rate, b_coef))
    ssm_old = update(*again).astype(BF16)

    near_rows = (
        (jnp.arange(2) ^ core)[:, None, None] * half
        + (jnp.arange(planes) ^ plane)[None, :, None] * chunk
        + jnp.arange(chunk)[None, None, :]
    ).reshape(-1)
    gated_all = jnp.concatenate(gather_pairs(gated_out, "expert"), axis=0)
    packed = pack_rows(
        send_rows, ssm_old, [(flip * move_cap, move_cap, tails[flip]) for flip in range(1, owners)]
    )
    gated_all, *packed = lax.optimization_barrier((gated_all, *packed))
    old_slots = new_slot.reshape(owners, row_count)
    near_slots = jnp.concatenate(
        [lax.dynamic_slice_in_dim(old_slots, own ^ flip, 1, axis=0) for flip in range(owners)], axis=0
    ).reshape(-1)
    order_hot = (near_rows[:, None] == near_slots[None, :]).astype(BF16)
    gated_new = jnp.dot(order_hot, gated_all, preferred_element_type=F32).astype(BF16)
    sent = jnp.dot(gated_new[half:], out_proj_weight, preferred_element_type=F32).astype(BF16)
    gated_half, sent = lax.optimization_barrier((gated_new[:half], sent))
    kept = jnp.dot(gated_half, out_proj_weight, preferred_element_type=F32)
    width = kept.shape[1]

    now = [swap(part, "expert", flip) for flip, part in enumerate(packed[:early], 1)]

    mix_half = kept + swap(sent, "dp", 1).astype(F32)
    gate_w, up_w, down_w = expert_gate[0], expert_up[0], expert_down[0]
    capacity = min(row_count, 5 * row_count * routes.shape[1] // (2 * owners))
    dense = capacity == row_count
    mix_chunk = scatter_pairs(list(mix_half.reshape(planes, chunk, width)), "dp", 2)
    residual_chunk = lax.dynamic_slice_in_dim(residual, core * half + plane * chunk, chunk, axis=0)
    stream_chunk = (residual_chunk.astype(F32) + mix_chunk).astype(BF16)
    stream_half = jnp.concatenate(gather_pairs(stream_chunk, "dp", 2), axis=0)
    stream_half, *now = lax.optimization_barrier((stream_half, *now))

    def in_order(near_half):
        stacked = near_half.reshape(planes, chunk, width)
        own_half = jnp.concatenate(
            [lax.dynamic_index_in_dim(stacked, plane ^ p, 0, keepdims=False) for p in range(planes)], axis=0
        )
        other = swap(own_half, "dp", 1)
        return jnp.where(
            core == 0, jnp.concatenate([own_half, other], axis=0), jnp.concatenate([other, own_half], axis=0)
        )

    def finish_states(later, now):
        ssm_new = place_rows(ssm_source, [ssm_old] + now + later)
        conv_rows = [conv_keep.reshape(row_count, -1)] + [
            part[-tail_rows:].reshape(move_cap, -1) for part in now + later
        ]
        conv_rows = jnp.concatenate(conv_rows, axis=0)
        conv_hot = (conv_source[:, None] == jnp.arange(conv_rows.shape[0])[None, :]).astype(BF16)
        conv_moved = jnp.dot(conv_hot, conv_rows, preferred_element_type=F32).astype(BF16)
        conv_new = jnp.concatenate(
            [conv_moved.reshape(row_count, tap_count - 2, channels), conv_input[:, None, :]], axis=1
        )
        return ssm_new, conv_new

    if not dense:
        later = [swap(part, "expert", flip) for flip, part in enumerate(packed[early:], early + 1)]
        stream = in_order(stream_half)
        layer_out = dispatch_experts(
            stream,
            norm_gain,
            routes,
            gate_weight,
            gate_w,
            up_w,
            down_w,
            row_count,
            capacity,
        )
        return (*finish_states(later, now), layer_out)

    blocks = gather_pairs(stream_half, "expert")
    gains = norm_gain.reshape(owners, 1, width)
    near_owners = jnp.arange(owners, dtype=jnp.int32) ^ own
    row_weight = jnp.sum(jnp.where(routes == own, gate_weight, 0.0), axis=1)
    near_weight = jnp.sum(
        jnp.where(near_rows[:, None] == jnp.arange(rows)[None, :], row_weight[None, :], 0.0), axis=1, keepdims=True
    )
    near_weight, blocks[0] = lax.optimization_barrier((near_weight, blocks[0]))
    pair = (blocks[0], swap(blocks[0], "dp", 1))
    sums = expert_kernel(near_owners, 0, [pair], gains, gate_w, up_w, near_weight)
    tied = lax.optimization_barrier((*blocks[1:], *packed[early:], *sums))
    pairs = [(block, swap(block, "dp", 1)) for block in tied[: owners - 1]]
    later = [swap(part, "expert", flip) for flip, part in enumerate(tied[owners - 1 : -3], early + 1)]
    outs = expert_kernel(near_owners, 1, pairs, gains, gate_w, up_w, near_weight, tied[-3:], down_w)

    others = [swap(outs[2 * k + 1], "dp", 1) for k in range(owners)]
    tied = lax.optimization_barrier((*others, *later))
    others, later = tied[:owners], list(tied[owners:])
    near_planes = planes // 2
    parts = add_pairs(outs[::2], others, near_planes * chunk)
    arrived = [swap(parts[2 * flip + 1], "expert", flip) for flip in range(1, owners)]
    arrived[0], *tied = lax.optimization_barrier((arrived[0], *later, *now))
    done = finish_states(list(tied[: len(later)]), list(tied[len(later) :]))
    *arrived, ssm_new, conv_new = lax.optimization_barrier((*arrived, *done))
    far_sum = parts[1].astype(F32) + sum(part.astype(F32) for part in arrived)
    far_rows = far_sum.astype(BF16).reshape(planes - near_planes, chunk, width)
    from_far = [
        swap(far_rows[k], "dp", 2 * (near_planes + k)).astype(F32) for k in range(planes - near_planes)
    ]
    arrived = [parts[0]] + [swap(parts[2 * flip], "expert", flip) for flip in range(1, owners)]
    tied = lax.optimization_barrier((*arrived, *from_far))
    arrived, from_far = tied[:owners], tied[owners:]
    near_sum = sum(part.astype(F32) for part in arrived).reshape(near_planes, chunk, width)
    mix_rows = scatter_pairs(list(near_sum), "dp", 2) + sum(from_far)
    layer_chunk = (stream_chunk.astype(F32) + mix_rows).astype(BF16)
    layer_half = jnp.concatenate(gather_pairs(layer_chunk, "dp", 2), axis=0)
    return (ssm_new, conv_new, in_order(layer_half))


def solution(mesh):
    in_specs = (
        P("expert", None, "dp"),
        P("expert", None, "dp"),
        P(),
        P("expert", "dp"),
        P("expert", "dp"),
        P(None, "dp"),
        P("dp"),
        P("dp", None),
        P(None, "dp"),
        P("dp"),
        P(None, "dp"),
        P("dp"),
        P("dp", "expert"),
        P(None, "expert"),
        P(),
        P(),
        P(),
        P("expert", None, "dp"),
        P("expert", None, "dp"),
        P("expert", "dp", None),
    )
    out_specs = (P("expert", None, "dp"), P("expert", None, "dp"), P(None, "expert"))
    return jax.shard_map(body, mesh=mesh, in_specs=in_specs, out_specs=out_specs, check_vma=False)
```

```python
import jax
import jax.numpy as jnp
from jax import lax
from jax.experimental import pallas as pl
from jax.experimental.pallas import tpu as pltpu
from jax.sharding import PartitionSpec as P

F32 = jnp.float32
BF16 = jnp.bfloat16


def swap(values, axis, flip):
    size = lax.axis_size(axis)
    return lax.ppermute(values, axis, [(i, i ^ flip) for i in range(size)])


def gather_pairs(values, axis, stride=1):
    count = lax.axis_size(axis) // stride
    return [values] + [swap(values, axis, flip * stride) for flip in range(1, count)]


def scatter_pairs(parts, axis, stride=1):
    total = parts[0].astype(F32)
    for flip in range(1, len(parts)):
        total = total + swap(parts[flip].astype(BF16), axis, flip * stride).astype(F32)
    return total


def dispatch_experts(stream, norm_gain, routes, gate_weight, expert_gate, expert_up, expert_down, row_count, capacity):
    owners = lax.axis_size("expert")
    top_count = routes.shape[1]
    width = stream.shape[1]
    expert_hot = (
        (routes[:, :, None] == jnp.arange(owners)[None, None, :])
        .astype(jnp.int32)
        .reshape(owners, row_count * top_count, owners)
    )
    prior = jnp.sum((jnp.cumsum(expert_hot, axis=1) - expert_hot) * expert_hot, axis=2)
    slot_of = (routes.reshape(owners, row_count * top_count) * capacity + prior).reshape(owners, row_count, top_count)
    matches = slot_of[:, :, :, None] == jnp.arange(owners * capacity)[None, None, None, :]
    dispatch_hot = jnp.any(matches, axis=2).astype(BF16).reshape(owners, row_count, owners, capacity)
    combine_w = jnp.sum(
        jnp.where(matches, gate_weight.reshape(owners, row_count, top_count)[:, :, :, None], 0.0), axis=2
    ).reshape(owners, row_count, owners, capacity)
    outgoing = jnp.einsum(
        "orec,ord->eocd", dispatch_hot, stream.reshape(owners, row_count, width), preferred_element_type=F32
    ).astype(BF16)
    arrived = lax.all_to_all(outgoing, "expert", split_axis=0, concat_axis=3, tiled=True)
    tokens = arrived.reshape(owners * capacity, -1).astype(F32)
    normed = (
        tokens * lax.rsqrt(jnp.mean(tokens * tokens, axis=1, keepdims=True) + 1e-05) * norm_gain[None, :]
    ).astype(BF16)
    gate_val = jnp.dot(normed, expert_gate, preferred_element_type=F32)
    up_val = jnp.dot(normed, expert_up, preferred_element_type=F32)
    hidden = (jax.nn.silu(gate_val) * up_val).astype(BF16)
    partial_out = jnp.dot(hidden, expert_down, preferred_element_type=F32).reshape(owners, capacity, -1)
    summed = lax.psum(partial_out, "dp")
    returned = lax.all_to_all(summed.astype(BF16), "expert", split_axis=2, concat_axis=0, tiled=True).astype(F32)
    expert_mix = jnp.einsum(
        "orec,eocd->ord",
        combine_w,
        returned.reshape(owners, owners, capacity, width),
        precision=lax.Precision.HIGHEST,
        preferred_element_type=F32,
    )
    return (stream.astype(F32) + expert_mix.reshape(-1, width)).astype(BF16)


def pack_rows(source_rows, states, segments):
    tails = [tail for _, _, tail in segments if tail is not None]
    extra = tails[0].shape[0]

    def kernel(rows_ref, states_ref, *refs):
        tail_refs, out_refs = list(refs[: len(tails)]), refs[len(tails) :]
        for (start, count, tail), out_ref in zip(segments, out_refs):

            def step(i, carry, start=start, out_ref=out_ref):
                out_ref[i] = states_ref[rows_ref[start + i]]
                return carry

            lax.fori_loop(0, count, step, 0, unroll=8)
            if tail is not None:
                out_ref[count:] = tail_refs.pop(0)[...]

    here = pl.BlockSpec(memory_space=pltpu.VMEM)
    return pl.pallas_call(
        kernel,
        out_shape=[
            jax.ShapeDtypeStruct((count + (0 if tail is None else extra),) + states.shape[1:], states.dtype)
            for _, count, tail in segments
        ],
        in_specs=[pl.BlockSpec(memory_space=pltpu.SMEM)] + [here] * (1 + len(tails)),
        out_specs=[here] * len(segments),
        name="pack_rows",
    )(source_rows, states, *tails)


def place_rows(source_rows, parts):
    counts = [part.shape[0] for part in parts]
    starts = [sum(counts[:k]) for k in range(len(parts))]
    row_shape = parts[0].shape[1:]
    row_count = source_rows.shape[0]

    def kernel(rows_ref, *refs):
        part_refs, (out_ref, held, sems) = refs[: len(parts)], refs[len(parts) :]
        copies = [
            pltpu.make_async_copy(part_ref, held.at[pl.ds(start, count)], sems.at[k])
            for k, (part_ref, start, count) in enumerate(zip(part_refs, starts, counts))
        ]
        for copy in copies:
            copy.start()
        for copy in copies:
            copy.wait()

        def step(i, carry):
            out_ref[i] = held[rows_ref[i]]
            return carry

        lax.fori_loop(0, row_count, step, 0, unroll=8)

    return pl.pallas_call(
        kernel,
        out_shape=jax.ShapeDtypeStruct((row_count,) + row_shape, parts[0].dtype),
        in_specs=[pl.BlockSpec(memory_space=pltpu.SMEM)] + [pl.BlockSpec(memory_space=pl.ANY)] * len(parts),
        out_specs=pl.BlockSpec(memory_space=pltpu.VMEM),
        scratch_shapes=[
            pltpu.VMEM((sum(counts),) + row_shape, parts[0].dtype),
            pltpu.SemaphoreType.DMA((len(parts),)),
        ],
        name="place_rows",
    )(source_rows, *[pltpu.with_memory_space_constraint(part, pltpu.HBM) for part in parts])


def expert_kernel(owner_ids, first, blocks, gains, gate_w, up_w, row_weight, carry=None, down_w=None):
    half, width = blocks[0][0].shape
    rows = 2 * half
    depth, hidden_dim = gate_w.shape
    count = len(blocks)
    tile = 256
    last = down_w is not None
    out_count = owner_ids.shape[0] if last else 0

    def kernel(ids_ref, *refs):
        block_refs, refs = refs[: 2 * count], refs[2 * count :]
        gains_ref, gate_ref, up_ref, weight_ref = refs[:4]
        refs = list(refs[4:])
        if carry is not None:
            gate_in, up_in, square_in = (refs.pop(0) for _ in range(3))
            gate_carry, up_carry, carry_sems = (refs.pop() for _ in range(3))
        if last:
            down_ref = refs.pop(0)
            out_refs = [refs.pop(0) for _ in range(2 * out_count)]
            hidden, down_buf, outs, tail_sems = (refs.pop() for _ in range(4))
        gate_sum, up_sum, square, raw, raw_sems, mixed, gate_buf, up_buf, sems = refs

        def fetch_block(b, h):
            return pltpu.make_async_copy(block_refs[2 * b + h], raw.at[b, h], raw_sems.at[b, h])

        def fetch(b, w):
            source, buf = ((gate_ref, gate_buf), (up_ref, up_buf))[w]
            at = pl.multiple_of(ids_ref[first + b] * width, width)
            return pltpu.make_async_copy(source.at[pl.ds(at, width)], buf.at[b], sems.at[b, w])

        def fetch_down(k):
            at = pl.multiple_of(ids_ref[k] * width, width)
            return pltpu.make_async_copy(down_ref.at[:, pl.ds(at, width)], down_buf.at[k], tail_sems.at[0, k])

        def fetch_carry(w):
            source, buf = ((gate_in, gate_carry), (up_in, up_carry))[w]
            return pltpu.make_async_copy(source, buf, carry_sems.at[w])

        def give(k, h):
            return pltpu.make_async_copy(outs.at[k, h], out_refs[2 * k + h], tail_sems.at[1 + h, k])

        queue = [[fetch(b, 0), fetch(b, 1)] for b in range(count)]
        if carry is not None:
            queue.append([fetch_carry(0), fetch_carry(1)])
        queue += [[fetch_down(k)] for k in range(out_count)]

        for b in range(count):
            fetch_block(b, 0).start()
            fetch_block(b, 1).start()

        def start_next():
            if queue:
                for copy in queue.pop(0):
                    copy.start()

        start_next()
        start_next()
        square[...] = jnp.zeros_like(square) if carry is None else square_in[...]
        for b in range(count):
            gain = gains_ref[ids_ref[first + b]]
            for h in range(2):
                fetch_block(b, h).wait()
                values = raw[b, h].astype(F32)
                square[h * half : (h + 1) * half] += jnp.sum(values * values, axis=1, keepdims=True)
                mixed[b, h * half : (h + 1) * half] = (values * gain).astype(BF16)
        for b in range(count):
            fetch(b, 0).wait()
            fetch(b, 1).wait()
            start_next()
            if carry is not None and b == count - 1:
                fetch_carry(0).wait()
                fetch_carry(1).wait()
                start_next()
            if last and b == count - 1:
                scale = lax.rsqrt(square[...] / depth + 1e-05)
            left = mixed[b]
            for at in range(0, hidden_dim, tile):
                to = min(at + tile, hidden_dim)
                gate_val = jnp.dot(left, gate_buf[b, :, at:to], preferred_element_type=F32)
                up_val = jnp.dot(left, up_buf[b, :, at:to], preferred_element_type=F32)
                if b > 0:
                    gate_val, up_val = gate_val + gate_sum[:, at:to], up_val + up_sum[:, at:to]
                if carry is not None and b == count - 1:
                    gate_val, up_val = gate_val + gate_carry[:, at:to], up_val + up_carry[:, at:to]
                if last and b == count - 1:
                    hidden[:, at:to] = (jax.nn.silu(gate_val * scale) * (up_val * scale)).astype(BF16)
                else:
                    gate_sum[:, at:to] = gate_val
                    up_sum[:, at:to] = up_val
        for k in range(out_count):
            fetch_down(k).wait()
            start_next()
            for at in range(0, width, tile):
                out = jnp.dot(hidden[...], down_buf[k, :, at : at + tile], preferred_element_type=F32)
                out = out * weight_ref[...]
                outs[k, 0, :, at : at + tile] = out[:half].astype(BF16)
                outs[k, 1, :, at : at + tile] = out[half:].astype(BF16)
            give(k, 0).start()
            give(k, 1).start()
        for k in range(out_count):
            give(k, 0).wait()
            give(k, 1).wait()

    here = pl.BlockSpec(memory_space=pltpu.VMEM)
    anywhere = pl.BlockSpec(memory_space=pl.ANY)
    operands = [owner_ids] + [part for block in blocks for part in block] + [gains, gate_w, up_w, row_weight]
    in_specs = [pl.BlockSpec(memory_space=pltpu.SMEM)] + [anywhere] * (2 * count) + [here, anywhere, anywhere, here]
    sums = [(rows, hidden_dim), (rows, hidden_dim), (rows, 1)]
    scratch = [
        pltpu.VMEM((count, 2, half, width), BF16),
        pltpu.SemaphoreType.DMA((count, 2)),
        pltpu.VMEM((count, rows, width), BF16),
        pltpu.VMEM((count, width, hidden_dim), BF16),
        pltpu.VMEM((count, width, hidden_dim), BF16),
        pltpu.SemaphoreType.DMA((count, 2)),
    ]
    if carry is not None:
        operands += list(carry)
        in_specs += [anywhere, anywhere, here]
    if last:
        operands += [down_w]
        in_specs += [anywhere]
        out_shape = [pltpu.HBM((half, width), BF16)] * (2 * out_count)
        out_specs = [pl.BlockSpec(memory_space=pltpu.HBM)] * (2 * out_count)
        scratch = [pltpu.VMEM(shape, F32) for shape in sums] + scratch
        scratch += [
            pltpu.SemaphoreType.DMA((3, out_count)),
            pltpu.VMEM((out_count, 2, half, width), BF16),
            pltpu.VMEM((out_count, hidden_dim, width), BF16),
            pltpu.VMEM((rows, hidden_dim), BF16),
        ]
    else:
        out_shape = [jax.ShapeDtypeStruct(shape, F32) for shape in sums]
        out_specs = [here] * 3
    if carry is not None:
        scratch += [
            pltpu.SemaphoreType.DMA((2,)),
            pltpu.VMEM((rows, hidden_dim), F32),
            pltpu.VMEM((rows, hidden_dim), F32),
        ]
    return pl.pallas_call(
        kernel,
        out_shape=out_shape,
        in_specs=in_specs,
        out_specs=out_specs,
        scratch_shapes=scratch,
        compiler_params=pltpu.CompilerParams(vmem_limit_bytes=50 * 1024 * 1024),
        name="expert_outputs" if last else "expert_sums",
    )(*operands)


def add_pairs(lefts, rights, cut):
    count = len(lefts)
    rows, width = lefts[0].shape

    def kernel(*refs):
        left_refs, right_refs, out_refs = refs[:count], refs[count : 2 * count], refs[2 * count : 4 * count]
        held, sums, in_sems, out_sems = refs[4 * count :]

        def take(k, w):
            return pltpu.make_async_copy((left_refs, right_refs)[w][k], held.at[k, w], in_sems.at[k, w])

        def give(k, w):
            part = sums.at[k, pl.ds(w * cut, rows - cut if w else cut)]
            return pltpu.make_async_copy(part, out_refs[2 * k + w], out_sems.at[k, w])

        order = range(count - 1, -1, -1)
        for k in order:
            take(k, 0).start()
            take(k, 1).start()
        for k in order:
            take(k, 0).wait()
            take(k, 1).wait()
            sums[k] = (held[k, 0].astype(F32) + held[k, 1].astype(F32)).astype(BF16)
            give(k, 0).start()
            give(k, 1).start()
        for k in order:
            give(k, 0).wait()
            give(k, 1).wait()

    anywhere = pl.BlockSpec(memory_space=pl.ANY)
    return pl.pallas_call(
        kernel,
        out_shape=[jax.ShapeDtypeStruct((size, width), BF16) for _ in lefts for size in (cut, rows - cut)],
        in_specs=[anywhere] * (2 * count),
        out_specs=[anywhere] * (2 * count),
        scratch_shapes=[
            pltpu.VMEM((count, 2, rows, width), BF16),
            pltpu.VMEM((count, rows, width), BF16),
            pltpu.SemaphoreType.DMA((count, 2)),
            pltpu.SemaphoreType.DMA((count, 2)),
        ],
        name="add_pairs",
    )(*lefts, *rights)


def body(
    ssm_state,
    conv_state,
    new_slot,
    conv_input,
    gate_input,
    conv_weight,
    conv_bias,
    x_proj_weight,
    step_weight,
    step_bias,
    decay_log,
    skip_gain,
    out_proj_weight,
    residual,
    norm_gain,
    routes,
    gate_weight,
    expert_gate,
    expert_up,
    expert_down,
):
    row_count, state_dim, channels = ssm_state.shape
    owners = lax.axis_size("expert")
    own = lax.axis_index("expert")
    dp_index = lax.axis_index("dp")
    core = dp_index % 2
    plane = dp_index // 2
    planes = lax.axis_size("dp") // 2
    rows = owners * row_count
    half = rows // 2
    chunk = half // planes
    tap_count = conv_weight.shape[0]

    last = swap(jnp.concatenate([conv_input, gate_input], axis=0), "expert", owners - 1)
    conv_all = jnp.concatenate(
        [conv_input] + [swap(conv_input, "expert", flip) for flip in range(1, owners - 1)] + [last[:row_count]], axis=0
    )
    my_slots = lax.dynamic_slice_in_dim(new_slot, own * row_count, row_count)
    near_ids = (
        (jnp.arange(owners) ^ own)[:, None] * row_count + jnp.arange(row_count)[None, :]
    ).reshape(-1)
    pick = (my_slots[:, None] == near_ids[None, :]).astype(BF16)
    conv_in = jnp.dot(pick, conv_all, preferred_element_type=F32)

    conv_sum = (
        jnp.sum(conv_state.astype(F32) * conv_weight[None, : tap_count - 1, :], axis=1)
        + conv_in * conv_weight[tap_count - 1][None, :]
        + conv_bias[None, :]
    )
    activated = jax.nn.silu(conv_sum).astype(BF16)
    projected = jnp.dot(activated, x_proj_weight, preferred_element_type=F32)
    projected = projected + swap(projected, "dp", 1)
    new_slot, my_slots, gate_input, projected = lax.optimization_barrier(
        (new_slot, my_slots, gate_input, projected)
    )
    gate_all = jnp.concatenate(
        [gate_input] + [swap(gate_input, "expert", flip) for flip in range(1, owners - 1)] + [last[row_count:]], axis=0
    )
    projected = scatter_pairs([projected] * planes, "dp", 2)

    move_cap = 2 * row_count // owners
    slot_count = owners * move_cap
    target = my_slots // row_count
    target_hot = (target[:, None] == jnp.arange(owners)[None, :]).astype(jnp.int32)
    earlier = jnp.sum((jnp.cumsum(target_hot, axis=0) - target_hot) * target_hot, axis=1)
    send_slot = (target ^ own) * move_cap + earlier
    send_match = jnp.arange(slot_count)[:, None] == send_slot[None, :]
    send_rows = jnp.sum(jnp.where(send_match, jnp.arange(row_count)[None, :], 0), axis=1)
    conv_keep = conv_state[:, 1:, :]
    conv_moving = jnp.dot(
        send_match.astype(BF16), conv_keep.reshape(row_count, -1), preferred_element_type=F32
    ).astype(BF16)
    tails = conv_moving.reshape(owners, -1, state_dim, channels)
    tail_rows = tails.shape[1]
    arriving = (new_slot // row_count == own).astype(jnp.int32).reshape(owners, row_count)
    arrive_rank = (jnp.cumsum(arriving, axis=1) - arriving).reshape(-1)
    source_flip = (jnp.arange(rows) // row_count) ^ own
    from_here = source_flip == 0
    here_row = jnp.arange(rows) % row_count
    is_source = new_slot[None, :] == (own * row_count + jnp.arange(row_count))[:, None]

    early = owners // 2

    def source_of(extra):
        at = row_count + (source_flip - 1) * (move_cap + extra) + arrive_rank
        return jnp.sum(jnp.where(is_source, jnp.where(from_here, here_row, at)[None, :], 0), axis=1)

    ssm_source = source_of(tail_rows)
    conv_source = source_of(0)

    rank_dim = step_weight.shape[0]
    step_low = projected[:, :rank_dim]
    b_coef = projected[:, rank_dim : rank_dim + state_dim]
    c_coef = projected[:, rank_dim + state_dim :]
    step_norm = (
        step_low * lax.rsqrt(jnp.mean(step_low * step_low, axis=1, keepdims=True) + 1e-06)
    ).astype(BF16)
    step_size = jax.nn.softplus(
        jnp.dot(step_norm, step_weight, preferred_element_type=F32) + step_bias[None, :]
    )
    act_float = activated.astype(F32)

    def update(state, step, rate, b_in):
        decays = jnp.exp(step[:, None, :] * rate[None, :, :])
        return decays * state.astype(F32) + (step * act_float)[:, None, :] * b_in[:, :, None]

    rate = -jnp.exp(decay_log)
    states = update(ssm_state, step_size, rate, b_coef)
    gate_in = jnp.dot(pick, gate_all, preferred_element_type=F32)
    gated_out = (
        (jnp.sum(c_coef[:, :, None] * states, axis=1) + skip_gain[None, :] * act_float) * jax.nn.silu(gate_in)
    ).astype(BF16)
    gated_out, *again = lax.optimization_barrier((gated_out, ssm_state, step_size, rate, b_coef))
    ssm_old = update(*again).astype(BF16)

    near_rows = (
        (jnp.arange(2) ^ core)[:, None, None] * half
        + (jnp.arange(planes) ^ plane)[None, :, None] * chunk
        + jnp.arange(chunk)[None, None, :]
    ).reshape(-1)
    gated_all = jnp.concatenate(gather_pairs(gated_out, "expert"), axis=0)
    packed = pack_rows(
        send_rows, ssm_old, [(flip * move_cap, move_cap, tails[flip]) for flip in range(1, owners)]
    )
    gated_all, *packed = lax.optimization_barrier((gated_all, *packed))
    old_slots = new_slot.reshape(owners, row_count)
    near_slots = jnp.concatenate(
        [lax.dynamic_slice_in_dim(old_slots, own ^ flip, 1, axis=0) for flip in range(owners)], axis=0
    ).reshape(-1)
    order_hot = (near_rows[:, None] == near_slots[None, :]).astype(BF16)
    gated_new = jnp.dot(order_hot, gated_all, preferred_element_type=F32).astype(BF16)
    sent = jnp.dot(gated_new[half:], out_proj_weight, preferred_element_type=F32).astype(BF16)
    gated_half, sent = lax.optimization_barrier((gated_new[:half], sent))
    kept = jnp.dot(gated_half, out_proj_weight, preferred_element_type=F32)
    width = kept.shape[1]

    now = [swap(part, "expert", flip) for flip, part in enumerate(packed[:early], 1)]

    mix_half = kept + swap(sent, "dp", 1).astype(F32)
    gate_w, up_w, down_w = expert_gate[0], expert_up[0], expert_down[0]
    capacity = min(row_count, 5 * row_count * routes.shape[1] // (2 * owners))
    dense = capacity == row_count
    mix_chunk = scatter_pairs(list(mix_half.reshape(planes, chunk, width)), "dp", 2)
    residual_chunk = lax.dynamic_slice_in_dim(residual, core * half + plane * chunk, chunk, axis=0)
    stream_chunk = (residual_chunk.astype(F32) + mix_chunk).astype(BF16)
    stream_half = jnp.concatenate(gather_pairs(stream_chunk, "dp", 2), axis=0)
    stream_half, *now = lax.optimization_barrier((stream_half, *now))

    def in_order(near_half):
        stacked = near_half.reshape(planes, chunk, width)
        own_half = jnp.concatenate(
            [lax.dynamic_index_in_dim(stacked, plane ^ p, 0, keepdims=False) for p in range(planes)], axis=0
        )
        other = swap(own_half, "dp", 1)
        return jnp.where(
            core == 0, jnp.concatenate([own_half, other], axis=0), jnp.concatenate([other, own_half], axis=0)
        )

    def finish_states(later, now):
        ssm_new = place_rows(ssm_source, [ssm_old] + now + later)
        conv_rows = [conv_keep.reshape(row_count, -1)] + [
            part[-tail_rows:].reshape(move_cap, -1) for part in now + later
        ]
        conv_rows = jnp.concatenate(conv_rows, axis=0)
        conv_hot = (conv_source[:, None] == jnp.arange(conv_rows.shape[0])[None, :]).astype(BF16)
        conv_moved = jnp.dot(conv_hot, conv_rows, preferred_element_type=F32).astype(BF16)
        conv_new = jnp.concatenate(
            [conv_moved.reshape(row_count, tap_count - 2, channels), conv_input[:, None, :]], axis=1
        )
        return ssm_new, conv_new

    if not dense:
        later = [swap(part, "expert", flip) for flip, part in enumerate(packed[early:], early + 1)]
        stream = in_order(stream_half)
        layer_out = dispatch_experts(
            stream,
            norm_gain,
            routes,
            gate_weight,
            gate_w,
            up_w,
            down_w,
            row_count,
            capacity,
        )
        return (*finish_states(later, now), layer_out)

    blocks = gather_pairs(stream_half, "expert")
    gains = norm_gain.reshape(owners, 1, width)
    near_owners = jnp.arange(owners, dtype=jnp.int32) ^ own
    row_weight = jnp.sum(jnp.where(routes == own, gate_weight, 0.0), axis=1)
    near_weight = jnp.sum(
        jnp.where(near_rows[:, None] == jnp.arange(rows)[None, :], row_weight[None, :], 0.0), axis=1, keepdims=True
    )
    near_weight, blocks[0] = lax.optimization_barrier((near_weight, blocks[0]))
    pair = (blocks[0], swap(blocks[0], "dp", 1))
    sums = expert_kernel(near_owners, 0, [pair], gains, gate_w, up_w, near_weight)
    tied = lax.optimization_barrier((*blocks[1:], *packed[early:], *sums))
    pairs = [(block, swap(block, "dp", 1)) for block in tied[: owners - 1]]
    later = [swap(part, "expert", flip) for flip, part in enumerate(tied[owners - 1 : -3], early + 1)]
    outs = expert_kernel(near_owners, 1, pairs, gains, gate_w, up_w, near_weight, tied[-3:], down_w)

    others = [swap(outs[2 * k + 1], "dp", 1) for k in range(owners)]
    tied = lax.optimization_barrier((*others, *later))
    others, later = tied[:owners], list(tied[owners:])
    near_planes = planes // 2
    parts = add_pairs(outs[::2], others, near_planes * chunk)
    arrived = [swap(parts[2 * flip + 1], "expert", flip) for flip in range(1, owners)]
    arrived[0], *tied = lax.optimization_barrier((arrived[0], *later, *now))
    done = finish_states(list(tied[: len(later)]), list(tied[len(later) :]))
    *arrived, ssm_new, conv_new = lax.optimization_barrier((*arrived, *done))
    far_sum = parts[1].astype(F32) + sum(part.astype(F32) for part in arrived)
    far_rows = far_sum.astype(BF16).reshape(planes - near_planes, chunk, width)
    from_far = [
        swap(far_rows[k], "dp", 2 * (near_planes + k)).astype(F32) for k in range(planes - near_planes)
    ]
    arrived = [parts[0]] + [swap(parts[2 * flip], "expert", flip) for flip in range(1, owners)]
    tied = lax.optimization_barrier((*arrived, *from_far))
    arrived, from_far = tied[:owners], tied[owners:]
    near_sum = sum(part.astype(F32) for part in arrived).reshape(near_planes, chunk, width)
    mix_rows = scatter_pairs(list(near_sum), "dp", 2) + sum(from_far)
    layer_chunk = (stream_chunk.astype(F32) + mix_rows).astype(BF16)
    layer_half = jnp.concatenate(gather_pairs(layer_chunk, "dp", 2), axis=0)
    return (ssm_new, conv_new, in_order(layer_half))


def solution(mesh):
    in_specs = (
        P("expert", None, "dp"),
        P("expert", None, "dp"),
        P(),
        P("expert", "dp"),
        P("expert", "dp"),
        P(None, "dp"),
        P("dp"),
        P("dp", None),
        P(None, "dp"),
        P("dp"),
        P(None, "dp"),
        P("dp"),
        P("dp", "expert"),
        P(None, "expert"),
        P(),
        P(),
        P(),
        P("expert", None, "dp"),
        P("expert", None, "dp"),
        P("expert", "dp", None),
    )
    out_specs = (P("expert", None, "dp"), P("expert", None, "dp"), P(None, "expert"))
    return jax.shard_map(body, mesh=mesh, in_specs=in_specs, out_specs=out_specs, check_vma=False)
```

```python
import jax
import jax.numpy as jnp
from jax import lax
from jax.experimental import pallas as pl
from jax.experimental.pallas import tpu as pltpu
from jax.sharding import PartitionSpec as P

F32 = jnp.float32
BF16 = jnp.bfloat16


def swap(values, axis, flip):
    size = lax.axis_size(axis)
    return lax.ppermute(values, axis, [(i, i ^ flip) for i in range(size)])


def gather_pairs(values, axis, stride=1):
    count = lax.axis_size(axis) // stride
    return [values] + [swap(values, axis, flip * stride) for flip in range(1, count)]


def scatter_pairs(parts, axis, stride=1):
    total = parts[0].astype(F32)
    for flip in range(1, len(parts)):
        total = total + swap(parts[flip].astype(BF16), axis, flip * stride).astype(F32)
    return total


def dispatch_experts(stream, norm_gain, routes, gate_weight, expert_gate, expert_up, expert_down, row_count, capacity):
    owners = lax.axis_size("expert")
    top_count = routes.shape[1]
    width = stream.shape[1]
    expert_hot = (
        (routes[:, :, None] == jnp.arange(owners)[None, None, :])
        .astype(jnp.int32)
        .reshape(owners, row_count * top_count, owners)
    )
    prior = jnp.sum((jnp.cumsum(expert_hot, axis=1) - expert_hot) * expert_hot, axis=2)
    slot_of = (routes.reshape(owners, row_count * top_count) * capacity + prior).reshape(owners, row_count, top_count)
    matches = slot_of[:, :, :, None] == jnp.arange(owners * capacity)[None, None, None, :]
    dispatch_hot = jnp.any(matches, axis=2).astype(BF16).reshape(owners, row_count, owners, capacity)
    combine_w = jnp.sum(
        jnp.where(matches, gate_weight.reshape(owners, row_count, top_count)[:, :, :, None], 0.0), axis=2
    ).reshape(owners, row_count, owners, capacity)
    outgoing = jnp.einsum(
        "orec,ord->eocd", dispatch_hot, stream.reshape(owners, row_count, width), preferred_element_type=F32
    ).astype(BF16)
    arrived = lax.all_to_all(outgoing, "expert", split_axis=0, concat_axis=3, tiled=True)
    tokens = arrived.reshape(owners * capacity, -1).astype(F32)
    normed = (
        tokens * lax.rsqrt(jnp.mean(tokens * tokens, axis=1, keepdims=True) + 1e-05) * norm_gain[None, :]
    ).astype(BF16)
    gate_val = jnp.dot(normed, expert_gate, preferred_element_type=F32)
    up_val = jnp.dot(normed, expert_up, preferred_element_type=F32)
    hidden = (jax.nn.silu(gate_val) * up_val).astype(BF16)
    partial_out = jnp.dot(hidden, expert_down, preferred_element_type=F32).reshape(owners, capacity, -1)
    summed = lax.psum(partial_out, "dp")
    returned = lax.all_to_all(summed.astype(BF16), "expert", split_axis=2, concat_axis=0, tiled=True).astype(F32)
    expert_mix = jnp.einsum(
        "orec,eocd->ord",
        combine_w,
        returned.reshape(owners, owners, capacity, width),
        precision=lax.Precision.HIGHEST,
        preferred_element_type=F32,
    )
    return (stream.astype(F32) + expert_mix.reshape(-1, width)).astype(BF16)


def pack_rows(source_rows, states, segments):
    tails = [tail for _, _, tail in segments if tail is not None]
    extra = tails[0].shape[0]

    def kernel(rows_ref, states_ref, *refs):
        tail_refs, out_refs = list(refs[: len(tails)]), refs[len(tails) :]
        for (start, count, tail), out_ref in zip(segments, out_refs):

            def step(i, carry, start=start, out_ref=out_ref):
                out_ref[i] = states_ref[rows_ref[start + i]]
                return carry

            lax.fori_loop(0, count, step, 0, unroll=8)
            if tail is not None:
                out_ref[count:] = tail_refs.pop(0)[...]

    here = pl.BlockSpec(memory_space=pltpu.VMEM)
    return pl.pallas_call(
        kernel,
        out_shape=[
            jax.ShapeDtypeStruct((count + (0 if tail is None else extra),) + states.shape[1:], states.dtype)
            for _, count, tail in segments
        ],
        in_specs=[pl.BlockSpec(memory_space=pltpu.SMEM)] + [here] * (1 + len(tails)),
        out_specs=[here] * len(segments),
        name="pack_rows",
    )(source_rows, states, *tails)


def place_rows(source_rows, parts):
    counts = [part.shape[0] for part in parts]
    starts = [sum(counts[:k]) for k in range(len(parts))]
    row_shape = parts[0].shape[1:]
    row_count = source_rows.shape[0]

    def kernel(rows_ref, *refs):
        part_refs, (out_ref, held, sems) = refs[: len(parts)], refs[len(parts) :]
        copies = [
            pltpu.make_async_copy(part_ref, held.at[pl.ds(start, count)], sems.at[k])
            for k, (part_ref, start, count) in enumerate(zip(part_refs, starts, counts))
        ]
        for copy in copies:
            copy.start()
        for copy in copies:
            copy.wait()

        def step(i, carry):
            out_ref[i] = held[rows_ref[i]]
            return carry

        lax.fori_loop(0, row_count, step, 0, unroll=8)

    return pl.pallas_call(
        kernel,
        out_shape=jax.ShapeDtypeStruct((row_count,) + row_shape, parts[0].dtype),
        in_specs=[pl.BlockSpec(memory_space=pltpu.SMEM)] + [pl.BlockSpec(memory_space=pl.ANY)] * len(parts),
        out_specs=pl.BlockSpec(memory_space=pltpu.VMEM),
        scratch_shapes=[
            pltpu.VMEM((sum(counts),) + row_shape, parts[0].dtype),
            pltpu.SemaphoreType.DMA((len(parts),)),
        ],
        name="place_rows",
    )(source_rows, *[pltpu.with_memory_space_constraint(part, pltpu.HBM) for part in parts])


def expert_kernel(owner_ids, first, blocks, gains, gate_w, up_w, row_weight, carry=None, down_w=None):
    half, width = blocks[0][0].shape
    rows = 2 * half
    depth, hidden_dim = gate_w.shape
    count = len(blocks)
    tile = 256
    last = down_w is not None
    out_count = owner_ids.shape[0] if last else 0

    def kernel(ids_ref, *refs):
        block_refs, refs = refs[: 2 * count], refs[2 * count :]
        gains_ref, gate_ref, up_ref, weight_ref = refs[:4]
        refs = list(refs[4:])
        if carry is not None:
            gate_in, up_in, square_in = (refs.pop(0) for _ in range(3))
            gate_carry, up_carry, carry_sems = (refs.pop() for _ in range(3))
        if last:
            down_ref = refs.pop(0)
            out_refs = [refs.pop(0) for _ in range(2 * out_count)]
            hidden, down_buf, outs, tail_sems = (refs.pop() for _ in range(4))
        gate_sum, up_sum, square, raw, raw_sems, mixed, gate_buf, up_buf, sems = refs

        def fetch_block(b, h):
            return pltpu.make_async_copy(block_refs[2 * b + h], raw.at[b, h], raw_sems.at[b, h])

        def fetch(b, w):
            source, buf = ((gate_ref, gate_buf), (up_ref, up_buf))[w]
            at = pl.multiple_of(ids_ref[first + b] * width, width)
            return pltpu.make_async_copy(source.at[pl.ds(at, width)], buf.at[b], sems.at[b, w])

        def fetch_down(k):
            at = pl.multiple_of(ids_ref[k] * width, width)
            return pltpu.make_async_copy(down_ref.at[:, pl.ds(at, width)], down_buf.at[k], tail_sems.at[0, k])

        def fetch_carry(w):
            source, buf = ((gate_in, gate_carry), (up_in, up_carry))[w]
            return pltpu.make_async_copy(source, buf, carry_sems.at[w])

        def give(k, h):
            return pltpu.make_async_copy(outs.at[k, h], out_refs[2 * k + h], tail_sems.at[1 + h, k])

        queue = [[fetch(b, 0), fetch(b, 1)] for b in range(count)]
        if carry is not None:
            queue.append([fetch_carry(0), fetch_carry(1)])
        queue += [[fetch_down(k)] for k in range(out_count)]

        for b in range(count):
            fetch_block(b, 0).start()
            fetch_block(b, 1).start()

        def start_next():
            if queue:
                for copy in queue.pop(0):
                    copy.start()

        start_next()
        start_next()
        square[...] = jnp.zeros_like(square) if carry is None else square_in[...]
        for b in range(count):
            gain = gains_ref[ids_ref[first + b]]
            for h in range(2):
                fetch_block(b, h).wait()
                values = raw[b, h].astype(F32)
                square[h * half : (h + 1) * half] += jnp.sum(values * values, axis=1, keepdims=True)
                mixed[b, h * half : (h + 1) * half] = (values * gain).astype(BF16)
        for b in range(count):
            fetch(b, 0).wait()
            fetch(b, 1).wait()
            start_next()
            if carry is not None and b == count - 1:
                fetch_carry(0).wait()
                fetch_carry(1).wait()
                start_next()
            if last and b == count - 1:
                scale = lax.rsqrt(square[...] / depth + 1e-05)
            left = mixed[b]
            for at in range(0, hidden_dim, tile):
                to = min(at + tile, hidden_dim)
                gate_val = jnp.dot(left, gate_buf[b, :, at:to], preferred_element_type=F32)
                up_val = jnp.dot(left, up_buf[b, :, at:to], preferred_element_type=F32)
                if b > 0:
                    gate_val, up_val = gate_val + gate_sum[:, at:to], up_val + up_sum[:, at:to]
                if carry is not None and b == count - 1:
                    gate_val, up_val = gate_val + gate_carry[:, at:to], up_val + up_carry[:, at:to]
                if last and b == count - 1:
                    hidden[:, at:to] = (jax.nn.silu(gate_val * scale) * (up_val * scale)).astype(BF16)
                else:
                    gate_sum[:, at:to] = gate_val
                    up_sum[:, at:to] = up_val
        for k in range(out_count):
            fetch_down(k).wait()
            start_next()
            for at in range(0, width, tile):
                out = jnp.dot(hidden[...], down_buf[k, :, at : at + tile], preferred_element_type=F32)
                out = out * weight_ref[...]
                outs[k, 0, :, at : at + tile] = out[:half].astype(BF16)
                outs[k, 1, :, at : at + tile] = out[half:].astype(BF16)
            give(k, 0).start()
            give(k, 1).start()
        for k in range(out_count):
            give(k, 0).wait()
            give(k, 1).wait()

    here = pl.BlockSpec(memory_space=pltpu.VMEM)
    anywhere = pl.BlockSpec(memory_space=pl.ANY)
    operands = [owner_ids] + [part for block in blocks for part in block] + [gains, gate_w, up_w, row_weight]
    in_specs = [pl.BlockSpec(memory_space=pltpu.SMEM)] + [anywhere] * (2 * count) + [here, anywhere, anywhere, here]
    sums = [(rows, hidden_dim), (rows, hidden_dim), (rows, 1)]
    scratch = [
        pltpu.VMEM((count, 2, half, width), BF16),
        pltpu.SemaphoreType.DMA((count, 2)),
        pltpu.VMEM((count, rows, width), BF16),
        pltpu.VMEM((count, width, hidden_dim), BF16),
        pltpu.VMEM((count, width, hidden_dim), BF16),
        pltpu.SemaphoreType.DMA((count, 2)),
    ]
    if carry is not None:
        operands += list(carry)
        in_specs += [anywhere, anywhere, here]
    if last:
        operands += [down_w]
        in_specs += [anywhere]
        out_shape = [pltpu.HBM((half, width), BF16)] * (2 * out_count)
        out_specs = [pl.BlockSpec(memory_space=pltpu.HBM)] * (2 * out_count)
        scratch = [pltpu.VMEM(shape, F32) for shape in sums] + scratch
        scratch += [
            pltpu.SemaphoreType.DMA((3, out_count)),
            pltpu.VMEM((out_count, 2, half, width), BF16),
            pltpu.VMEM((out_count, hidden_dim, width), BF16),
            pltpu.VMEM((rows, hidden_dim), BF16),
        ]
    else:
        out_shape = [jax.ShapeDtypeStruct(shape, F32) for shape in sums]
        out_specs = [here] * 3
    if carry is not None:
        scratch += [
            pltpu.SemaphoreType.DMA((2,)),
            pltpu.VMEM((rows, hidden_dim), F32),
            pltpu.VMEM((rows, hidden_dim), F32),
        ]
    return pl.pallas_call(
        kernel,
        out_shape=out_shape,
        in_specs=in_specs,
        out_specs=out_specs,
        scratch_shapes=scratch,
        compiler_params=pltpu.CompilerParams(vmem_limit_bytes=50 * 1024 * 1024),
        name="expert_outputs" if last else "expert_sums",
    )(*operands)


def add_pairs(lefts, rights, cut):
    count = len(lefts)
    rows, width = lefts[0].shape

    def kernel(*refs):
        left_refs, right_refs, out_refs = refs[:count], refs[count : 2 * count], refs[2 * count : 4 * count]
        held, sums, in_sems, out_sems = refs[4 * count :]

        def take(k, w):
            return pltpu.make_async_copy((left_refs, right_refs)[w][k], held.at[k, w], in_sems.at[k, w])

        def give(k, w):
            part = sums.at[k, pl.ds(w * cut, rows - cut if w else cut)]
            return pltpu.make_async_copy(part, out_refs[2 * k + w], out_sems.at[k, w])

        order = range(count - 1, -1, -1)
        for k in order:
            take(k, 0).start()
            take(k, 1).start()
        for k in order:
            take(k, 0).wait()
            take(k, 1).wait()
            sums[k] = (held[k, 0].astype(F32) + held[k, 1].astype(F32)).astype(BF16)
            give(k, 0).start()
            give(k, 1).start()
        for k in order:
            give(k, 0).wait()
            give(k, 1).wait()

    anywhere = pl.BlockSpec(memory_space=pl.ANY)
    return pl.pallas_call(
        kernel,
        out_shape=[jax.ShapeDtypeStruct((size, width), BF16) for _ in lefts for size in (cut, rows - cut)],
        in_specs=[anywhere] * (2 * count),
        out_specs=[anywhere] * (2 * count),
        scratch_shapes=[
            pltpu.VMEM((count, 2, rows, width), BF16),
            pltpu.VMEM((count, rows, width), BF16),
            pltpu.SemaphoreType.DMA((count, 2)),
            pltpu.SemaphoreType.DMA((count, 2)),
        ],
        name="add_pairs",
    )(*lefts, *rights)


def body(
    ssm_state,
    conv_state,
    new_slot,
    conv_input,
    gate_input,
    conv_weight,
    conv_bias,
    x_proj_weight,
    step_weight,
    step_bias,
    decay_log,
    skip_gain,
    out_proj_weight,
    residual,
    norm_gain,
    routes,
    gate_weight,
    expert_gate,
    expert_up,
    expert_down,
):
    row_count, state_dim, channels = ssm_state.shape
    owners = lax.axis_size("expert")
    own = lax.axis_index("expert")
    dp_index = lax.axis_index("dp")
    core = dp_index % 2
    plane = dp_index // 2
    planes = lax.axis_size("dp") // 2
    rows = owners * row_count
    half = rows // 2
    chunk = half // planes
    tap_count = conv_weight.shape[0]

    last = swap(jnp.concatenate([conv_input, gate_input], axis=0), "expert", owners - 1)
    conv_all = jnp.concatenate(
        [conv_input] + [swap(conv_input, "expert", flip) for flip in range(1, owners - 1)] + [last[:row_count]], axis=0
    )
    my_slots = lax.dynamic_slice_in_dim(new_slot, own * row_count, row_count)
    near_ids = (
        (jnp.arange(owners) ^ own)[:, None] * row_count + jnp.arange(row_count)[None, :]
    ).reshape(-1)
    pick = (my_slots[:, None] == near_ids[None, :]).astype(BF16)
    conv_in = jnp.dot(pick, conv_all, preferred_element_type=F32)

    conv_sum = (
        jnp.sum(conv_state.astype(F32) * conv_weight[None, : tap_count - 1, :], axis=1)
        + conv_in * conv_weight[tap_count - 1][None, :]
        + conv_bias[None, :]
    )
    activated = jax.nn.silu(conv_sum).astype(BF16)
    projected = jnp.dot(activated, x_proj_weight, preferred_element_type=F32)
    projected = projected + swap(projected, "dp", 1)
    new_slot, my_slots, gate_input, projected = lax.optimization_barrier(
        (new_slot, my_slots, gate_input, projected)
    )
    gate_all = jnp.concatenate(
        [gate_input] + [swap(gate_input, "expert", flip) for flip in range(1, owners - 1)] + [last[row_count:]], axis=0
    )
    projected = scatter_pairs([projected] * planes, "dp", 2)

    move_cap = 2 * row_count // owners
    slot_count = owners * move_cap
    target = my_slots // row_count
    target_hot = (target[:, None] == jnp.arange(owners)[None, :]).astype(jnp.int32)
    earlier = jnp.sum((jnp.cumsum(target_hot, axis=0) - target_hot) * target_hot, axis=1)
    send_slot = (target ^ own) * move_cap + earlier
    send_match = jnp.arange(slot_count)[:, None] == send_slot[None, :]
    send_rows = jnp.sum(jnp.where(send_match, jnp.arange(row_count)[None, :], 0), axis=1)
    conv_keep = conv_state[:, 1:, :]
    conv_moving = jnp.dot(
        send_match.astype(BF16), conv_keep.reshape(row_count, -1), preferred_element_type=F32
    ).astype(BF16)
    tails = conv_moving.reshape(owners, -1, state_dim, channels)
    tail_rows = tails.shape[1]
    arriving = (new_slot // row_count == own).astype(jnp.int32).reshape(owners, row_count)
    arrive_rank = (jnp.cumsum(arriving, axis=1) - arriving).reshape(-1)
    source_flip = (jnp.arange(rows) // row_count) ^ own
    from_here = source_flip == 0
    here_row = jnp.arange(rows) % row_count
    is_source = new_slot[None, :] == (own * row_count + jnp.arange(row_count))[:, None]

    early = owners // 2

    def source_of(extra):
        at = row_count + (source_flip - 1) * (move_cap + extra) + arrive_rank
        return jnp.sum(jnp.where(is_source, jnp.where(from_here, here_row, at)[None, :], 0), axis=1)

    ssm_source = source_of(tail_rows)
    conv_source = source_of(0)

    rank_dim = step_weight.shape[0]
    step_low = projected[:, :rank_dim]
    b_coef = projected[:, rank_dim : rank_dim + state_dim]
    c_coef = projected[:, rank_dim + state_dim :]
    step_norm = (
        step_low * lax.rsqrt(jnp.mean(step_low * step_low, axis=1, keepdims=True) + 1e-06)
    ).astype(BF16)
    step_size = jax.nn.softplus(
        jnp.dot(step_norm, step_weight, preferred_element_type=F32) + step_bias[None, :]
    )
    act_float = activated.astype(F32)

    def update(state, step, rate, b_in):
        decays = jnp.exp(step[:, None, :] * rate[None, :, :])
        return decays * state.astype(F32) + (step * act_float)[:, None, :] * b_in[:, :, None]

    rate = -jnp.exp(decay_log)
    states = update(ssm_state, step_size, rate, b_coef)
    gate_in = jnp.dot(pick, gate_all, preferred_element_type=F32)
    gated_out = (
        (jnp.sum(c_coef[:, :, None] * states, axis=1) + skip_gain[None, :] * act_float) * jax.nn.silu(gate_in)
    ).astype(BF16)
    gated_out, *again = lax.optimization_barrier((gated_out, ssm_state, step_size, rate, b_coef))
    ssm_old = update(*again).astype(BF16)

    near_rows = (
        (jnp.arange(2) ^ core)[:, None, None] * half
        + (jnp.arange(planes) ^ plane)[None, :, None] * chunk
        + jnp.arange(chunk)[None, None, :]
    ).reshape(-1)
    gated_all = jnp.concatenate(gather_pairs(gated_out, "expert"), axis=0)
    packed = pack_rows(
        send_rows, ssm_old, [(flip * move_cap, move_cap, tails[flip]) for flip in range(1, owners)]
    )
    gated_all, *packed = lax.optimization_barrier((gated_all, *packed))
    old_slots = new_slot.reshape(owners, row_count)
    near_slots = jnp.concatenate(
        [lax.dynamic_slice_in_dim(old_slots, own ^ flip, 1, axis=0) for flip in range(owners)], axis=0
    ).reshape(-1)
    order_hot = (near_rows[:, None] == near_slots[None, :]).astype(BF16)
    gated_new = jnp.dot(order_hot, gated_all, preferred_element_type=F32).astype(BF16)
    sent = jnp.dot(gated_new[half:], out_proj_weight, preferred_element_type=F32).astype(BF16)
    gated_half, sent = lax.optimization_barrier((gated_new[:half], sent))
    kept = jnp.dot(gated_half, out_proj_weight, preferred_element_type=F32)
    width = kept.shape[1]

    now = [swap(part, "expert", flip) for flip, part in enumerate(packed[:early], 1)]

    mix_half = kept + swap(sent, "dp", 1).astype(F32)
    gate_w, up_w, down_w = expert_gate[0], expert_up[0], expert_down[0]
    capacity = min(row_count, 5 * row_count * routes.shape[1] // (2 * owners))
    dense = capacity == row_count
    mix_chunk = scatter_pairs(list(mix_half.reshape(planes, chunk, width)), "dp", 2)
    residual_chunk = lax.dynamic_slice_in_dim(residual, core * half + plane * chunk, chunk, axis=0)
    stream_chunk = (residual_chunk.astype(F32) + mix_chunk).astype(BF16)
    stream_half = jnp.concatenate(gather_pairs(stream_chunk, "dp", 2), axis=0)
    stream_half, *now = lax.optimization_barrier((stream_half, *now))

    def in_order(near_half):
        stacked = near_half.reshape(planes, chunk, width)
        own_half = jnp.concatenate(
            [lax.dynamic_index_in_dim(stacked, plane ^ p, 0, keepdims=False) for p in range(planes)], axis=0
        )
        other = swap(own_half, "dp", 1)
        return jnp.where(
            core == 0, jnp.concatenate([own_half, other], axis=0), jnp.concatenate([other, own_half], axis=0)
        )

    def finish_states(later, now):
        ssm_new = place_rows(ssm_source, [ssm_old] + now + later)
        conv_rows = [conv_keep.reshape(row_count, -1)] + [
            part[-tail_rows:].reshape(move_cap, -1) for part in now + later
        ]
        conv_rows = jnp.concatenate(conv_rows, axis=0)
        conv_hot = (conv_source[:, None] == jnp.arange(conv_rows.shape[0])[None, :]).astype(BF16)
        conv_moved = jnp.dot(conv_hot, conv_rows, preferred_element_type=F32).astype(BF16)
        conv_new = jnp.concatenate(
            [conv_moved.reshape(row_count, tap_count - 2, channels), conv_input[:, None, :]], axis=1
        )
        return ssm_new, conv_new

    if not dense:
        later = [swap(part, "expert", flip) for flip, part in enumerate(packed[early:], early + 1)]
        stream = in_order(stream_half)
        layer_out = dispatch_experts(
            stream,
            norm_gain,
            routes,
            gate_weight,
            gate_w,
            up_w,
            down_w,
            row_count,
            capacity,
        )
        return (*finish_states(later, now), layer_out)

    blocks = gather_pairs(stream_half, "expert")
    gains = norm_gain.reshape(owners, 1, width)
    near_owners = jnp.arange(owners, dtype=jnp.int32) ^ own
    row_weight = jnp.sum(jnp.where(routes == own, gate_weight, 0.0), axis=1)
    near_weight = jnp.sum(
        jnp.where(near_rows[:, None] == jnp.arange(rows)[None, :], row_weight[None, :], 0.0), axis=1, keepdims=True
    )
    near_weight, blocks[0] = lax.optimization_barrier((near_weight, blocks[0]))
    pair = (blocks[0], swap(blocks[0], "dp", 1))
    sums = expert_kernel(near_owners, 0, [pair], gains, gate_w, up_w, near_weight)
    tied = lax.optimization_barrier((*blocks[1:], *packed[early:], *sums))
    pairs = [(block, swap(block, "dp", 1)) for block in tied[: owners - 1]]
    later = [swap(part, "expert", flip) for flip, part in enumerate(tied[owners - 1 : -3], early + 1)]
    outs = expert_kernel(near_owners, 1, pairs, gains, gate_w, up_w, near_weight, tied[-3:], down_w)

    others = [swap(outs[2 * k + 1], "dp", 1) for k in range(owners)]
    tied = lax.optimization_barrier((*others, *later))
    others, later = tied[:owners], list(tied[owners:])
    near_planes = planes // 2
    parts = add_pairs(outs[::2], others, near_planes * chunk)
    arrived = [swap(parts[2 * flip + 1], "expert", flip) for flip in range(1, owners)]
    arrived[0], *tied = lax.optimization_barrier((arrived[0], *later, *now))
    done = finish_states(list(tied[: len(later)]), list(tied[len(later) :]))
    *arrived, ssm_new = lax.optimization_barrier((*arrived, done[0]))
    far_sum = parts[1].astype(F32) + sum(part.astype(F32) for part in arrived)
    far_rows = far_sum.astype(BF16).reshape(planes - near_planes, chunk, width)
    from_far = [
        swap(far_rows[k], "dp", 2 * (near_planes + k)).astype(F32) for k in range(planes - near_planes)
    ]
    arrived = [parts[0]] + [swap(parts[2 * flip], "expert", flip) for flip in range(1, owners)]
    *tied, conv_new = lax.optimization_barrier((*arrived, *from_far, done[1]))
    arrived, from_far = tied[:owners], tied[owners:]
    near_sum = sum(part.astype(F32) for part in arrived).reshape(near_planes, chunk, width)
    mix_rows = scatter_pairs(list(near_sum), "dp", 2) + sum(from_far)
    layer_chunk = (stream_chunk.astype(F32) + mix_rows).astype(BF16)
    layer_half = jnp.concatenate(gather_pairs(layer_chunk, "dp", 2), axis=0)
    return (ssm_new, conv_new, in_order(layer_half))


def solution(mesh):
    in_specs = (
        P("expert", None, "dp"),
        P("expert", None, "dp"),
        P(),
        P("expert", "dp"),
        P("expert", "dp"),
        P(None, "dp"),
        P("dp"),
        P("dp", None),
        P(None, "dp"),
        P("dp"),
        P(None, "dp"),
        P("dp"),
        P("dp", "expert"),
        P(None, "expert"),
        P(),
        P(),
        P(),
        P("expert", None, "dp"),
        P("expert", None, "dp"),
        P("expert", "dp", None),
    )
    out_specs = (P("expert", None, "dp"), P("expert", None, "dp"), P(None, "expert"))
    return jax.shard_map(body, mesh=mesh, in_specs=in_specs, out_specs=out_specs, check_vma=False)
```
